32 devices in a mesh: dp: 8 (over z, x), tensor: 4 (over y, core).
Axes of the slice: x: 2, y: 2, z: 4, core: 2. Of those that a mesh axis runs over, the one named last changes fastest.
Arguments:
- activations: bfloat16 [3072, 8192], P('dp', 'tensor'), may hold values from -6 to 6
- basis: bfloat16 [8192, 256], replicated, may hold values from -0.0625 to 0.0625
- out_grad: bfloat16 [3072, 14592], P('dp', 'tensor'), may hold values from -0.15625 to 0.15625
- first_moment: float32 [4, 3648, 256], P('tensor', 'dp'), may hold values from -6 to 6
- second_moment: float32 [4, 3648, 256], P('tensor', 'dp'), may hold values from 0.02 to 0.5
Outputs:
- new_first_moment: float32 [4, 3648, 256], P('tensor', 'dp')
- new_second_moment: float32 [4, 3648, 256], P('tensor', 'dp')
- full_update: bfloat16 [4, 3648, 8192], P('tensor', 'dp')
The draws below stay inside these ranges and needn't reach their ends.
All inputs are finite; a program needn't handle non-finite values.
Results may differ from the reference program's by a relative error of at most 0.005.
Values may be sent and summed in bfloat16 or wider, within the bound.
No kernel may reach another device: no remote copies, remote signals or barrier semaphores. Data moves between devices by JAX's collectives and lax.ppermute only.
A program may use at most 64 MiB of HBM per device.

```python
import math
import jax
import jax.numpy as jnp
from jax import lax

D = 8192
FF = 14592
R = 256
STEP = 100
TOKENS = 3072
FF_T = 3648
N_TENSOR = 4


def raised(result, stream_key, source, target, blocks, factor):
    def block_of(dim):
        return (jnp.arange(result.shape[dim]) // (result.shape[dim] // blocks)).reshape((-1,) + (1,) * (result.ndim - 1 - dim))

    near = jax.random.permutation(stream_key, blocks)[block_of(target)]
    far = (block_of(target) + blocks // 2) % blocks
    return jnp.where((block_of(source) == near) | (block_of(source) == far), factor * result, result)


def shard_levels(key, dims, split, low, top_value):
    def one(axis_at, blocks):
        steps = jax.random.uniform(jax.random.fold_in(jax.random.fold_in(key, 6), axis_at), (blocks,), jnp.float32, low / len(split), top_value / len(split))
        return jnp.repeat(jnp.exp(steps), dims[axis_at] // blocks).reshape((-1,) + (1,) * (len(dims) - axis_at - 1))

    loudness = one(*split[0])
    for cut in split[1:]:
        loudness = loudness * one(*cut)
    return loudness


def centred(stream_key, extent, width, bound, cuts=(), dtype=jnp.bfloat16):
    factor_of = shard_levels(stream_key, extent, cuts, -0.22, 0.18) if cuts else 1.0
    drawn = jax.random.normal(stream_key, extent, jnp.float32) * width * factor_of
    return jnp.minimum(jnp.maximum(drawn, -bound), bound).astype(dtype)


def bell_draw_with(stream_key, dims, scale, limit, pieces, heavy, held_as=jnp.bfloat16):
    drawn = scale * jax.random.normal(stream_key, dims, jnp.float32)
    if pieces:
        drawn = drawn * shard_levels(stream_key, dims, pieces, -0.22, 0.18)
    return jnp.clip(raised(drawn, jax.random.fold_in(stream_key, 3), *heavy), -limit, limit).astype(held_as)


def setup_inputs(seed: int = 0) -> dict:
    key_of = jax.random.split(jax.random.key(seed), 6)
    return {
        "activations": centred(key_of[0], (TOKENS, D), 1.0, 6.0, ((0, 8), (1, 4))),
        "basis": centred(key_of[1], (D, R), D ** -0.5, 0.0625),
        "out_grad": bell_draw_with(key_of[2], (TOKENS, FF), (TOKENS ** -0.5), 0.15625, ((0, 8), (1, 4)), (0, 1, 8, 2.0)),
        "first_moment": centred(key_of[3], (N_TENSOR, FF_T, R), 1.0, 6.0, ((0, 4), (1, 8)), jnp.float32),
        "second_moment": jnp.clip(jnp.exp(math.log(0.5) - 3.218876 * jax.random.uniform(key_of[4], (N_TENSOR, FF_T, R), jnp.float32) ** shard_levels(key_of[4], (N_TENSOR, FF_T, R), ((0, 4), (1, 8)), -0.2, 0.2)), 0.02, 0.5),
    }


def reference(activations, basis, out_grad, first_moment, second_moment):
    coded_rows = jnp.dot(activations, basis, preferred_element_type=jnp.float32).astype(jnp.bfloat16)
    coded_grad = lax.dot_general(out_grad, coded_rows, (((0,), (0,)), ((), ())), preferred_element_type=jnp.float32)
    coded_grad = coded_grad.reshape(N_TENSOR, FF // N_TENSOR, R)
    new_first = 0.9 * first_moment + 0.1 * coded_grad
    new_second = 0.999 * second_moment + 0.001 * coded_grad * coded_grad
    first_hat = new_first / (1.0 - 0.9 ** STEP)
    second_hat = new_second / (1.0 - 0.999 ** STEP)
    direction = (first_hat / (jnp.sqrt(second_hat) + 1e-08)).astype(jnp.bfloat16)
    update = lax.dot_general(direction.reshape(FF, R), basis, (((1,), (1,)), ((), ())), preferred_element_type=jnp.float32)
    full_update = update.astype(jnp.bfloat16).reshape(N_TENSOR, FF // N_TENSOR, D)
    return (new_first, new_second, full_update)
```

```python
import functools

import jax
import jax.numpy as jnp
from jax import lax
from jax.experimental import pallas as pl
from jax.experimental.pallas import tpu as pltpu
from jax.sharding import PartitionSpec as P

STEP = 100
BF = jnp.bfloat16
F32 = jnp.float32


def swap(value, axis, bit, count):
    return lax.ppermute(value, axis, [(i, i ^ bit) for i in range(count)])


DEEP = 4


def partial_code_kernel(activations, basis, keep, send, act_buf, basis_buf, total, sems):
    feats = activations.shape[1]
    start = lax.axis_index("tensor") * feats
    step = feats // DEEP
    copies = []
    for k in range(DEEP):
        copies.append(
            pltpu.make_async_copy(
                basis.at[pl.ds(pl.multiple_of(start + k * step, step), step), :],
                basis_buf.at[k],
                sems.at[0, k],
            )
        )
        copies.append(
            pltpu.make_async_copy(
                activations.at[:, pl.ds(k * step, step)], act_buf.at[k], sems.at[1, k]
            )
        )
    for copy in copies:
        copy.start()
    for k in range(DEEP):
        copies[2 * k].wait()
        copies[2 * k + 1].wait()
        part = jnp.dot(act_buf[k], basis_buf[k], preferred_element_type=F32)
        total[...] = part if k == 0 else total[...] + part
    half = keep.shape[0]
    core = lax.rem(lax.axis_index("tensor"), 2)
    keep[...] = total[pl.ds(pl.multiple_of(core * half, half), half), :]
    send[...] = total[pl.ds(pl.multiple_of((1 - core) * half, half), half), :].astype(BF)


def partial_code(activations, basis):
    rows, feats = activations.shape
    rank = basis.shape[1]
    vmem = pl.BlockSpec(memory_space=pltpu.VMEM)
    hbm = pl.BlockSpec(memory_space=pltpu.HBM)
    return pl.pallas_call(
        partial_code_kernel,
        out_shape=(
            jax.ShapeDtypeStruct((rows // 2, rank), F32),
            jax.ShapeDtypeStruct((rows // 2, rank), BF),
        ),
        in_specs=[hbm, hbm],
        out_specs=(vmem, vmem),
        scratch_shapes=[
            pltpu.VMEM((DEEP, rows, feats // DEEP), BF),
            pltpu.VMEM((DEEP, feats // DEEP, rank), BF),
            pltpu.VMEM((rows, rank), F32),
            pltpu.SemaphoreType.DMA((2, DEEP)),
        ],
        compiler_params=pltpu.CompilerParams(vmem_limit_bytes=53 * 2**20),
        cost_estimate=pl.CostEstimate(
            flops=2 * rows * feats * rank,
            bytes_accessed=2 * feats * (rows + rank),
            transcendentals=0,
        ),
        name="partial_code",
    )(activations, basis)


def coded_total(keep, send, n_tensor):
    core = lax.axis_index("tensor") % 2
    total = keep + swap(send, "tensor", 1, n_tensor).astype(F32)
    bit = 2
    while bit < n_tensor:
        total = total + swap(total.astype(BF), "tensor", bit, n_tensor).astype(F32)
        bit *= 2
    mine = total.astype(BF)
    theirs = swap(mine, "tensor", 1, n_tensor)
    return jnp.where(
        core == 0,
        jnp.concatenate([mine, theirs], 0),
        jnp.concatenate([theirs, mine], 0),
    )


def line_total(grad_rows, coded, n_dp, cuts, spare=8):
    rows = grad_rows.shape[0] // n_dp
    d = lax.axis_index("dp")
    z, x = d // 2, d % 2
    first, second = cuts

    def both(block, code, cut):
        split = grad_rows.reshape(n_dp, rows, -1)
        part = lax.dynamic_slice_in_dim(split, block * 2, 2, 0)[:, cut[0] : cut[1]]
        return lax.dot_general(
            part, code, (((2,), (0,)), ((), ())), preferred_element_type=F32
        )

    def term(block, side, code, cut=(0, rows)):
        start = (block * 2 + side) * rows + cut[0]
        part = lax.dynamic_slice_in_dim(grad_rows, start, cut[1] - cut[0], 0)
        return jnp.dot(part, code, preferred_element_type=F32)

    def parity(value, side):
        return lax.dynamic_index_in_dim(value, side, 0, False).astype(F32)

    def hop(value, bit):
        full = [(i, i ^ (2 * bit)) for i in range(n_dp)]
        return lax.ppermute(value.astype(BF), "dp", full)

    def pair(value):
        return swap(value.astype(BF), "dp", 1, n_dp)

    def piece(value, cut):
        return value[cut[0] : cut[1]].astype(F32)

    def padded(value):
        return jnp.pad(value, ((0, rows - value.shape[0]), (0, 0)))

    got2 = pair(term(z ^ 2, 1 - x, coded))
    near1 = hop(both(z ^ 1, coded, (0, first[1] + spare)), 1)
    got3 = pair(term(z ^ 3, 1 - x, coded))

    sums = [(term(z ^ 2, x, coded, cut) + piece(got2, cut)).astype(BF) for cut in cuts]
    code, sums = lax.optimization_barrier((coded, sums))
    passed = [hop(part, 1) for part in sums]
    out1 = term(z ^ 1, 1 - x, code, second).astype(BF)
    code, out1, near1 = lax.optimization_barrier((code, out1, near1))
    got1 = pair(out1)
    near1 = near1[:, : first[1]]
    own_in = (term(z, 1 - x, code) + padded(parity(near1, 1 - x))).astype(BF)
    code, own_in = lax.optimization_barrier((coded, own_in))
    own = pair(own_in)
    far = []
    for cut, part in zip(cuts, passed):
        total = term(z ^ 3, x, code, cut) + piece(got3, cut) + part.astype(F32)
        code, total = lax.optimization_barrier((code, total.astype(BF)))
        far.append(hop(total, 3))
    late = hop(term(z ^ 1, x, code, second) + got1.astype(F32), 1)
    kept = [term(z, x, code, first) + parity(near1, x), term(z, x, code, second)]
    return kept, own, [(far[0],), (far[1], late)]


WIDE = 2048


def adam_update_kernel(cut, n_terms, n_olds, own, got, first, second, basis, *refs):
    terms, refs = refs[:n_terms], refs[n_terms + n_olds :]
    new_first, new_second, update = refs[:3]
    first_buf, second_buf, direction, blocks, moment_sem, block_sem = refs[3:]
    here = pl.ds(cut[0], cut[1] - cut[0])
    grad = own[...] + got[here, :].astype(F32)
    for term in terms:
        grad = grad + term[...].astype(F32)
    first_buf[...] = 0.9 * first[here, :] + 0.1 * grad
    second_buf[...] = 0.999 * second[here, :] + 0.001 * grad * grad
    moments = [
        pltpu.make_async_copy(first_buf, new_first.at[here, :], moment_sem.at[0]),
        pltpu.make_async_copy(second_buf, new_second.at[here, :], moment_sem.at[1]),
    ]
    for copy in moments:
        copy.start()
    first_hat = first_buf[...] / (1.0 - 0.9**STEP)
    second_hat = second_buf[...] / (1.0 - 0.999**STEP)
    direction[...] = (first_hat / (jnp.sqrt(second_hat) + 1e-08)).astype(BF)

    def out_copy(j):
        return pltpu.make_async_copy(
            blocks.at[j], update.at[here, pl.ds(j * WIDE, WIDE)], block_sem.at[j]
        )

    count = basis.shape[0] // WIDE
    for j in range(count):
        part = lax.dot_general(
            direction[...],
            basis[pl.ds(j * WIDE, WIDE), :],
            (((1,), (1,)), ((), ())),
            preferred_element_type=F32,
        )
        blocks[j] = part.astype(BF)
        out_copy(j).start()
    for j in range(count):
        out_copy(j).wait()
    for copy in moments:
        copy.wait()


def adam_update(cut, own, got, terms, first, second, basis, olds):
    rows, rank = first.shape
    feats = basis.shape[0]
    here = cut[1] - cut[0]
    vmem = pl.BlockSpec(memory_space=pltpu.VMEM)
    hbm = pl.BlockSpec(memory_space=pl.ANY)
    n_inputs = 5 + len(terms)
    return pl.pallas_call(
        functools.partial(adam_update_kernel, cut, len(terms), len(olds)),
        out_shape=(
            jax.ShapeDtypeStruct((rows, rank), F32),
            jax.ShapeDtypeStruct((rows, rank), F32),
            jax.ShapeDtypeStruct((rows, feats), BF),
        ),
        in_specs=[vmem] * n_inputs + [hbm] * len(olds),
        out_specs=(hbm, hbm, hbm),
        input_output_aliases={n_inputs + i: i for i in range(len(olds))},
        scratch_shapes=[
            pltpu.VMEM((here, rank), F32),
            pltpu.VMEM((here, rank), F32),
            pltpu.VMEM((here, rank), BF),
            pltpu.VMEM((feats // WIDE, here, WIDE), BF),
            pltpu.SemaphoreType.DMA((2,)),
            pltpu.SemaphoreType.DMA((feats // WIDE,)),
        ],
        compiler_params=pltpu.CompilerParams(vmem_limit_bytes=24 * 2**20),
        cost_estimate=pl.CostEstimate(
            flops=2 * here * rank * feats,
            bytes_accessed=2 * here * feats + 2 * rank * feats,
            transcendentals=here * rank,
        ),
        name="adam_update",
    )(own, got, first, second, basis, *terms, *olds)


def on_device(activations, basis, out_grad, first_moment, second_moment):
    n_tensor = lax.axis_size("tensor")
    n_dp = lax.axis_size("dp")
    keep, send = partial_code(activations, basis)
    coded_rows = coded_total(keep, send, n_tensor)
    if n_dp == 8:
        rows = first_moment.shape[1]
        middle = rows // 32 * 16
        cuts = ((0, middle), (middle, rows))
        kept, got, fars = line_total(out_grad.T, coded_rows, n_dp, cuts)
        outs = ()
        for cut, own, terms in zip(cuts, kept, fars):
            outs = adam_update(
                cut, own, got, terms, first_moment[0], second_moment[0], basis, outs
            )
        return tuple(out[None] for out in outs)
    term = jnp.dot(out_grad.T, coded_rows, preferred_element_type=F32)
    coded_grad = lax.psum_scatter(term, "dp", scatter_dimension=0, tiled=True)[None]
    new_first = 0.9 * first_moment + 0.1 * coded_grad
    new_second = 0.999 * second_moment + 0.001 * coded_grad * coded_grad
    first_hat = new_first / (1.0 - 0.9**STEP)
    second_hat = new_second / (1.0 - 0.999**STEP)
    direction = (first_hat / (jnp.sqrt(second_hat) + 1e-08)).astype(BF)
    update = lax.dot_general(
        direction[0], basis, (((1,), (1,)), ((), ())), preferred_element_type=F32
    )
    return (new_first, new_second, update.astype(BF)[None])


def solution(mesh):
    placed = (
        P("dp", "tensor"),
        P(),
        P("dp", "tensor"),
        P("tensor", "dp", None),
        P("tensor", "dp", None),
    )
    return jax.shard_map(
        on_device,
        mesh=mesh,
        in_specs=placed,
        out_specs=(P("tensor", "dp", None), P("tensor", "dp", None), P("tensor", "dp", None)),
        check_vma=False,
    )
```

```python
import functools

import jax
import jax.numpy as jnp
from jax import lax
from jax.experimental import pallas as pl
from jax.experimental.pallas import tpu as pltpu
from jax.sharding import PartitionSpec as P

STEP = 100
BF = jnp.bfloat16
F32 = jnp.float32


def swap(value, axis, bit, count):
    return lax.ppermute(value, axis, [(i, i ^ bit) for i in range(count)])


DEEP = 4


def partial_code_kernel(activations, basis, keep, send, act_buf, basis_buf, total, sems):
    feats = activations.shape[1]
    start = lax.axis_index("tensor") * feats
    step = feats // DEEP
    copies = []
    for k in range(DEEP):
        copies.append(
            pltpu.make_async_copy(
                basis.at[pl.ds(pl.multiple_of(start + k * step, step), step), :],
                basis_buf.at[k],
                sems.at[0, k],
            )
        )
        copies.append(
            pltpu.make_async_copy(
                activations.at[:, pl.ds(k * step, step)], act_buf.at[k], sems.at[1, k]
            )
        )
    for copy in copies:
        copy.start()
    for k in range(DEEP):
        copies[2 * k].wait()
        copies[2 * k + 1].wait()
        part = jnp.dot(act_buf[k], basis_buf[k], preferred_element_type=F32)
        total[...] = part if k == 0 else total[...] + part
    half = keep.shape[0]
    core = lax.rem(lax.axis_index("tensor"), 2)
    keep[...] = total[pl.ds(pl.multiple_of(core * half, half), half), :]
    send[...] = total[pl.ds(pl.multiple_of((1 - core) * half, half), half), :].astype(BF)


def partial_code(activations, basis):
    rows, feats = activations.shape
    rank = basis.shape[1]
    vmem = pl.BlockSpec(memory_space=pltpu.VMEM)
    hbm = pl.BlockSpec(memory_space=pltpu.HBM)
    return pl.pallas_call(
        partial_code_kernel,
        out_shape=(
            jax.ShapeDtypeStruct((rows // 2, rank), F32),
            jax.ShapeDtypeStruct((rows // 2, rank), BF),
        ),
        in_specs=[hbm, hbm],
        out_specs=(vmem, vmem),
        scratch_shapes=[
            pltpu.VMEM((DEEP, rows, feats // DEEP), BF),
            pltpu.VMEM((DEEP, feats // DEEP, rank), BF),
            pltpu.VMEM((rows, rank), F32),
            pltpu.SemaphoreType.DMA((2, DEEP)),
        ],
        compiler_params=pltpu.CompilerParams(vmem_limit_bytes=53 * 2**20),
        cost_estimate=pl.CostEstimate(
            flops=2 * rows * feats * rank,
            bytes_accessed=2 * feats * (rows + rank),
            transcendentals=0,
        ),
        name="partial_code",
    )(activations, basis)


def coded_total(keep, send, n_tensor):
    core = lax.axis_index("tensor") % 2
    total = keep + swap(send, "tensor", 1, n_tensor).astype(F32)
    bit = 2
    while bit < n_tensor:
        total = total + swap(total.astype(BF), "tensor", bit, n_tensor).astype(F32)
        bit *= 2
    mine = total.astype(BF)
    theirs = swap(mine, "tensor", 1, n_tensor)
    return jnp.where(
        core == 0,
        jnp.concatenate([mine, theirs], 0),
        jnp.concatenate([theirs, mine], 0),
    )


def line_total(grad_rows, coded, n_dp, cuts, spare=8):
    rows = grad_rows.shape[0] // n_dp
    d = lax.axis_index("dp")
    z, x = d // 2, d % 2
    first, second = cuts

    def both(block, code, cut):
        split = grad_rows.reshape(n_dp, rows, -1)
        part = lax.dynamic_slice_in_dim(split, block * 2, 2, 0)[:, cut[0] : cut[1]]
        return lax.dot_general(
            part, code, (((2,), (0,)), ((), ())), preferred_element_type=F32
        )

    def term(block, side, code, cut=(0, rows)):
        start = (block * 2 + side) * rows + cut[0]
        part = lax.dynamic_slice_in_dim(grad_rows, start, cut[1] - cut[0], 0)
        return jnp.dot(part, code, preferred_element_type=F32)

    def parity(value, side):
        return lax.dynamic_index_in_dim(value, side, 0, False).astype(F32)

    def hop(value, bit):
        full = [(i, i ^ (2 * bit)) for i in range(n_dp)]
        return lax.ppermute(value.astype(BF), "dp", full)

    def pair(value):
        return swap(value.astype(BF), "dp", 1, n_dp)

    def piece(value, cut):
        return value[cut[0] : cut[1]].astype(F32)

    def padded(value):
        return jnp.pad(value, ((0, rows - value.shape[0]), (0, 0)))

    got2 = pair(term(z ^ 2, 1 - x, coded))
    out1 = both(z ^ 1, coded, (0, first[1] + spare)).astype(BF)
    code, out1 = lax.optimization_barrier((coded, out1))
    near1 = hop(out1, 1)
    got3 = pair(term(z ^ 3, 1 - x, code))

    sums = [(term(z ^ 2, x, coded, cut) + piece(got2, cut)).astype(BF) for cut in cuts]
    code, sums = lax.optimization_barrier((coded, sums))
    passed = [hop(part, 1) for part in sums]
    out1 = term(z ^ 1, 1 - x, code, second).astype(BF)
    code, out1, near1 = lax.optimization_barrier((code, out1, near1))
    got1 = pair(out1)
    near1 = near1[:, : first[1]]
    own_in = (term(z, 1 - x, code) + padded(parity(near1, 1 - x))).astype(BF)
    code, own_in = lax.optimization_barrier((coded, own_in))
    own = pair(own_in)
    def total(cut, part, code):
        value = term(z ^ 3, x, code, cut) + piece(got3, cut) + part.astype(F32)
        return lax.optimization_barrier((code, value.astype(BF)))

    code, total_a = total(first, passed[0], code)
    far_a = hop(total_a, 3)
    late = (term(z ^ 1, x, code, second) + got1.astype(F32)).astype(BF)
    code, late = lax.optimization_barrier((code, late))
    late = hop(late, 1)
    code, total_b = total(second, passed[1], code)
    far_b = hop(total_b, 3)
    kept = [term(z, x, code, first) + parity(near1, x), term(z, x, code, second)]
    return kept, own, [(far_a,), (late, far_b)]


WIDE = 512


def adam_update_kernel(cut, n_terms, n_olds, own, got, first, second, basis, *refs):
    terms, refs = refs[:n_terms], refs[n_terms + n_olds :]
    new_first, new_second, update = refs[:3]
    first_buf, second_buf, direction, blocks, moment_sem, block_sem = refs[3:]
    here = pl.ds(cut[0], cut[1] - cut[0])
    grad = own[...] + got[here, :].astype(F32)
    for term in terms:
        grad = grad + term[...].astype(F32)
    first_buf[...] = 0.9 * first[here, :] + 0.1 * grad
    second_buf[...] = 0.999 * second[here, :] + 0.001 * grad * grad
    moments = [
        pltpu.make_async_copy(first_buf, new_first.at[here, :], moment_sem.at[0]),
        pltpu.make_async_copy(second_buf, new_second.at[here, :], moment_sem.at[1]),
    ]
    for copy in moments:
        copy.start()
    first_hat = first_buf[...] / (1.0 - 0.9**STEP)
    second_hat = second_buf[...] / (1.0 - 0.999**STEP)
    direction[...] = (first_hat / (jnp.sqrt(second_hat) + 1e-08)).astype(BF)

    def out_copy(j):
        return pltpu.make_async_copy(
            blocks.at[j], update.at[here, pl.ds(j * WIDE, WIDE)], block_sem.at[j]
        )

    count = basis.shape[0] // WIDE
    for j in range(count):
        part = lax.dot_general(
            direction[...],
            basis[pl.ds(j * WIDE, WIDE), :],
            (((1,), (1,)), ((), ())),
            preferred_element_type=F32,
        )
        blocks[j] = part.astype(BF)
        out_copy(j).start()
    for j in range(count):
        out_copy(j).wait()
    for copy in moments:
        copy.wait()


def adam_update(cut, own, got, terms, first, second, basis, olds):
    rows, rank = first.shape
    feats = basis.shape[0]
    here = cut[1] - cut[0]
    vmem = pl.BlockSpec(memory_space=pltpu.VMEM)
    hbm = pl.BlockSpec(memory_space=pl.ANY)
    n_inputs = 5 + len(terms)
    return pl.pallas_call(
        functools.partial(adam_update_kernel, cut, len(terms), len(olds)),
        out_shape=(
            jax.ShapeDtypeStruct((rows, rank), F32),
            jax.ShapeDtypeStruct((rows, rank), F32),
            jax.ShapeDtypeStruct((rows, feats), BF),
        ),
        in_specs=[vmem] * n_inputs + [hbm] * len(olds),
        out_specs=(hbm, hbm, hbm),
        input_output_aliases={n_inputs + i: i for i in range(len(olds))},
        scratch_shapes=[
            pltpu.VMEM((here, rank), F32),
            pltpu.VMEM((here, rank), F32),
            pltpu.VMEM((here, rank), BF),
            pltpu.VMEM((feats // WIDE, here, WIDE), BF),
            pltpu.SemaphoreType.DMA((2,)),
            pltpu.SemaphoreType.DMA((feats // WIDE,)),
        ],
        compiler_params=pltpu.CompilerParams(vmem_limit_bytes=24 * 2**20),
        cost_estimate=pl.CostEstimate(
            flops=2 * here * rank * feats,
            bytes_accessed=2 * here * feats + 2 * rank * feats,
            transcendentals=here * rank,
        ),
        name="adam_update",
    )(own, got, first, second, basis, *terms, *olds)


def on_device(activations, basis, out_grad, first_moment, second_moment):
    n_tensor = lax.axis_size("tensor")
    n_dp = lax.axis_size("dp")
    keep, send = partial_code(activations, basis)
    coded_rows = coded_total(keep, send, n_tensor)
    if n_dp == 8:
        rows = first_moment.shape[1]
        middle = rows // 32 * 16
        cuts = ((0, middle), (middle, rows))
        kept, got, fars = line_total(out_grad.T, coded_rows, n_dp, cuts)
        outs = ()
        for cut, own, terms in zip(cuts, kept, fars):
            outs = adam_update(
                cut, own, got, terms, first_moment[0], second_moment[0], basis, outs
            )
        return tuple(out[None] for out in outs)
    term = jnp.dot(out_grad.T, coded_rows, preferred_element_type=F32)
    coded_grad = lax.psum_scatter(term, "dp", scatter_dimension=0, tiled=True)[None]
    new_first = 0.9 * first_moment + 0.1 * coded_grad
    new_second = 0.999 * second_moment + 0.001 * coded_grad * coded_grad
    first_hat = new_first / (1.0 - 0.9**STEP)
    second_hat = new_second / (1.0 - 0.999**STEP)
    direction = (first_hat / (jnp.sqrt(second_hat) + 1e-08)).astype(BF)
    update = lax.dot_general(
        direction[0], basis, (((1,), (1,)), ((), ())), preferred_element_type=F32
    )
    return (new_first, new_second, update.astype(BF)[None])


def solution(mesh):
    placed = (
        P("dp", "tensor"),
        P(),
        P("dp", "tensor"),
        P("tensor", "dp", None),
        P("tensor", "dp", None),
    )
    return jax.shard_map(
        on_device,
        mesh=mesh,
        in_specs=placed,
        out_specs=(P("tensor", "dp", None), P("tensor", "dp", None), P("tensor", "dp", None)),
        check_vma=False,
    )
```

```python
import functools

import jax
import jax.numpy as jnp
from jax import lax
from jax.experimental import pallas as pl
from jax.experimental.pallas import tpu as pltpu
from jax.sharding import PartitionSpec as P

STEP = 100
BF = jnp.bfloat16
F32 = jnp.float32


def swap(value, axis, bit, count):
    return lax.ppermute(value, axis, [(i, i ^ bit) for i in range(count)])


DEEP = 4


def partial_code_kernel(activations, basis, keep, send, act_buf, basis_buf, total, sems):
    feats = activations.shape[1]
    start = lax.axis_index("tensor") * feats
    step = feats // DEEP
    copies = []
    for k in range(DEEP):
        copies.append(
            pltpu.make_async_copy(
                basis.at[pl.ds(pl.multiple_of(start + k * step, step), step), :],
                basis_buf.at[k],
                sems.at[0, k],
            )
        )
        copies.append(
            pltpu.make_async_copy(
                activations.at[:, pl.ds(k * step, step)], act_buf.at[k], sems.at[1, k]
            )
        )
    for copy in copies:
        copy.start()
    for k in range(DEEP):
        copies[2 * k].wait()
        copies[2 * k + 1].wait()
        part = jnp.dot(act_buf[k], basis_buf[k], preferred_element_type=F32)
        total[...] = part if k == 0 else total[...] + part
    half = keep.shape[0]
    core = lax.rem(lax.axis_index("tensor"), 2)
    keep[...] = total[pl.ds(pl.multiple_of(core * half, half), half), :]
    send[...] = total[pl.ds(pl.multiple_of((1 - core) * half, half), half), :].astype(BF)


def partial_code(activations, basis):
    rows, feats = activations.shape
    rank = basis.shape[1]
    vmem = pl.BlockSpec(memory_space=pltpu.VMEM)
    hbm = pl.BlockSpec(memory_space=pltpu.HBM)
    return pl.pallas_call(
        partial_code_kernel,
        out_shape=(
            jax.ShapeDtypeStruct((rows // 2, rank), F32),
            jax.ShapeDtypeStruct((rows // 2, rank), BF),
        ),
        in_specs=[hbm, hbm],
        out_specs=(vmem, vmem),
        scratch_shapes=[
            pltpu.VMEM((DEEP, rows, feats // DEEP), BF),
            pltpu.VMEM((DEEP, feats // DEEP, rank), BF),
            pltpu.VMEM((rows, rank), F32),
            pltpu.SemaphoreType.DMA((2, DEEP)),
        ],
        compiler_params=pltpu.CompilerParams(vmem_limit_bytes=53 * 2**20),
        cost_estimate=pl.CostEstimate(
            flops=2 * rows * feats * rank,
            bytes_accessed=2 * feats * (rows + rank),
            transcendentals=0,
        ),
        name="partial_code",
    )(activations, basis)


PARTS = 8


def transposed_kernel(source, target, parts, sems):
    rows = parts.shape[1]
    copies = [
        pltpu.make_async_copy(source.at[pl.ds(k * rows, rows), :], parts.at[k], sems.at[k])
        for k in range(PARTS)
    ]
    for copy in copies:
        copy.start()
    for k in range(PARTS):
        copies[k].wait()
        target[:, pl.ds(k * rows, rows)] = parts[k].T


def transposed(array):
    rows, cols = array.shape
    return pl.pallas_call(
        transposed_kernel,
        out_shape=jax.ShapeDtypeStruct((cols, rows), array.dtype),
        in_specs=[pl.BlockSpec(memory_space=pltpu.HBM)],
        out_specs=pl.BlockSpec(memory_space=pltpu.VMEM),
        scratch_shapes=[
            pltpu.VMEM((PARTS, rows // PARTS, cols), array.dtype),
            pltpu.SemaphoreType.DMA((PARTS,)),
        ],
        compiler_params=pltpu.CompilerParams(vmem_limit_bytes=48 * 2**20),
        cost_estimate=pl.CostEstimate(
            flops=0, bytes_accessed=4 * array.size, transcendentals=0
        ),
        name="transposed",
    )(array)


def coded_total(keep, send, n_tensor):
    core = lax.axis_index("tensor") % 2
    total = keep + swap(send, "tensor", 1, n_tensor).astype(F32)
    bit = 2
    while bit < n_tensor:
        total = total + swap(total.astype(BF), "tensor", bit, n_tensor).astype(F32)
        bit *= 2
    mine = total.astype(BF)
    theirs = swap(mine, "tensor", 1, n_tensor)
    return jnp.where(
        core == 0,
        jnp.concatenate([mine, theirs], 0),
        jnp.concatenate([theirs, mine], 0),
    )


def line_total(grad_rows, coded, basis, n_dp, cuts, spare=8):
    rows = grad_rows.shape[0] // n_dp
    d = lax.axis_index("dp")
    z, x = d // 2, d % 2
    first, second = cuts

    def both(block, code, cut):
        split = grad_rows.reshape(n_dp, rows, -1)
        part = lax.dynamic_slice_in_dim(split, block * 2, 2, 0)[:, cut[0] : cut[1]]
        return lax.dot_general(
            part, code, (((2,), (0,)), ((), ())), preferred_element_type=F32
        )

    def term(block, side, code, cut=(0, rows)):
        start = (block * 2 + side) * rows + cut[0]
        part = lax.dynamic_slice_in_dim(grad_rows, start, cut[1] - cut[0], 0)
        return jnp.dot(part, code, preferred_element_type=F32)

    def parity(value, side):
        return lax.dynamic_index_in_dim(value, side, 0, False).astype(F32)

    def hop(value, bit):
        full = [(i, i ^ (2 * bit)) for i in range(n_dp)]
        return lax.ppermute(value.astype(BF), "dp", full)

    def pair(value):
        return swap(value.astype(BF), "dp", 1, n_dp)

    def piece(value, cut):
        return value[cut[0] : cut[1]].astype(F32)

    def padded(value):
        return jnp.pad(value, ((0, rows - value.shape[0]), (0, 0)))

    got2 = pair(term(z ^ 2, 1 - x, coded))
    out1 = both(z ^ 1, coded, (0, first[1] + spare)).astype(BF)
    code, out1 = lax.optimization_barrier((coded, out1))
    near1 = hop(out1, 1)
    out3 = term(z ^ 3, 1 - x, code).astype(BF)
    out3, basis = lax.optimization_barrier((out3, basis))
    got3 = pair(out3)
    basis_t = transposed(basis)
    coded, basis_t = lax.optimization_barrier((coded, basis_t))

    sums = [(term(z ^ 2, x, coded, cut) + piece(got2, cut)).astype(BF) for cut in cuts]
    code, sums = lax.optimization_barrier((coded, sums))
    passed = [hop(part, 1) for part in sums]
    out1 = term(z ^ 1, 1 - x, code, second).astype(BF)
    code, out1, near1 = lax.optimization_barrier((code, out1, near1))
    got1 = pair(out1)
    near1 = near1[:, : first[1]]
    own_in = (term(z, 1 - x, code) + padded(parity(near1, 1 - x))).astype(BF)
    code, own_in = lax.optimization_barrier((coded, own_in))
    own = pair(own_in)
    def total(cut, part, code):
        value = term(z ^ 3, x, code, cut) + piece(got3, cut) + part.astype(F32)
        return lax.optimization_barrier((code, value.astype(BF)))

    code, total_a = total(first, passed[0], code)
    far_a = hop(total_a, 3)
    code, total_b = total(second, passed[1], code)
    far_b = hop(total_b, 3)
    late = hop(term(z ^ 1, x, code, second) + got1.astype(F32), 1)
    kept = [term(z, x, code, first) + parity(near1, x), term(z, x, code, second)]
    return kept, own, [(far_a,), (far_b, late)], basis_t


WIDE = 512


def adam_update_kernel(cut, n_terms, n_olds, own, got, first, second, basis_t, *refs):
    terms, refs = refs[:n_terms], refs[n_terms + n_olds :]
    new_first, new_second, update = refs[:3]
    first_buf, second_buf, direction, blocks, moment_sem, block_sem = refs[3:]
    here = pl.ds(cut[0], cut[1] - cut[0])
    grad = own[...] + got[here, :].astype(F32)
    for term in terms:
        grad = grad + term[...].astype(F32)
    first_buf[...] = 0.9 * first[here, :] + 0.1 * grad
    second_buf[...] = 0.999 * second[here, :] + 0.001 * grad * grad
    moments = [
        pltpu.make_async_copy(first_buf, new_first.at[here, :], moment_sem.at[0]),
        pltpu.make_async_copy(second_buf, new_second.at[here, :], moment_sem.at[1]),
    ]
    for copy in moments:
        copy.start()
    first_hat = first_buf[...] / (1.0 - 0.9**STEP)
    second_hat = second_buf[...] / (1.0 - 0.999**STEP)
    direction[...] = (first_hat / (jnp.sqrt(second_hat) + 1e-08)).astype(BF)

    def out_copy(j):
        return pltpu.make_async_copy(
            blocks.at[j], update.at[here, pl.ds(j * WIDE, WIDE)], block_sem.at[j]
        )

    count = basis_t.shape[1] // WIDE
    for j in range(count):
        part = jnp.dot(
            direction[...],
            basis_t[:, pl.ds(j * WIDE, WIDE)],
            preferred_element_type=F32,
        )
        blocks[j] = part.astype(BF)
        out_copy(j).start()
    for j in range(count):
        out_copy(j).wait()
    for copy in moments:
        copy.wait()


def adam_update(cut, own, got, terms, first, second, basis_t, olds):
    rows, rank = first.shape
    feats = basis_t.shape[1]
    here = cut[1] - cut[0]
    vmem = pl.BlockSpec(memory_space=pltpu.VMEM)
    hbm = pl.BlockSpec(memory_space=pl.ANY)
    n_inputs = 5 + len(terms)
    return pl.pallas_call(
        functools.partial(adam_update_kernel, cut, len(terms), len(olds)),
        out_shape=(
            jax.ShapeDtypeStruct((rows, rank), F32),
            jax.ShapeDtypeStruct((rows, rank), F32),
            jax.ShapeDtypeStruct((rows, feats), BF),
        ),
        in_specs=[vmem] * n_inputs + [hbm] * len(olds),
        out_specs=(hbm, hbm, hbm),
        input_output_aliases={n_inputs + i: i for i in range(len(olds))},
        scratch_shapes=[
            pltpu.VMEM((here, rank), F32),
            pltpu.VMEM((here, rank), F32),
            pltpu.VMEM((here, rank), BF),
            pltpu.VMEM((feats // WIDE, here, WIDE), BF),
            pltpu.SemaphoreType.DMA((2,)),
            pltpu.SemaphoreType.DMA((feats // WIDE,)),
        ],
        compiler_params=pltpu.CompilerParams(vmem_limit_bytes=24 * 2**20),
        cost_estimate=pl.CostEstimate(
            flops=2 * here * rank * feats,
            bytes_accessed=2 * here * feats + 2 * rank * feats,
            transcendentals=here * rank,
        ),
        name="adam_update",
    )(own, got, first, second, basis_t, *terms, *olds)


def on_device(activations, basis, out_grad, first_moment, second_moment):
    n_tensor = lax.axis_size("tensor")
    n_dp = lax.axis_size("dp")
    keep, send = partial_code(activations, basis)
    coded_rows = coded_total(keep, send, n_tensor)
    grad_rows = out_grad.T
    if n_dp == 8:
        rows = first_moment.shape[1]
        middle = rows // 32 * 16
        cuts = ((0, middle), (middle, rows))
        kept, got, fars, basis_t = line_total(grad_rows, coded_rows, basis, n_dp, cuts)
        outs = ()
        for cut, own, terms in zip(cuts, kept, fars):
            outs = adam_update(
                cut, own, got, terms, first_moment[0], second_moment[0], basis_t, outs
            )
        return tuple(out[None] for out in outs)
    term = jnp.dot(grad_rows, coded_rows, preferred_element_type=F32)
    coded_grad = lax.psum_scatter(term, "dp", scatter_dimension=0, tiled=True)[None]
    new_first = 0.9 * first_moment + 0.1 * coded_grad
    new_second = 0.999 * second_moment + 0.001 * coded_grad * coded_grad
    first_hat = new_first / (1.0 - 0.9**STEP)
    second_hat = new_second / (1.0 - 0.999**STEP)
    direction = (first_hat / (jnp.sqrt(second_hat) + 1e-08)).astype(BF)
    update = lax.dot_general(
        direction[0], basis, (((1,), (1,)), ((), ())), preferred_element_type=F32
    )
    return (new_first, new_second, update.astype(BF)[None])


def solution(mesh):
    placed = (
        P("dp", "tensor"),
        P(),
        P("dp", "tensor"),
        P("tensor", "dp", None),
        P("tensor", "dp", None),
    )
    return jax.shard_map(
        on_device,
        mesh=mesh,
        in_specs=placed,
        out_specs=(P("tensor", "dp", None), P("tensor", "dp", None), P("tensor", "dp", None)),
        check_vma=False,
    )
```

```python
import functools

import jax
import jax.numpy as jnp
from jax import lax
from jax.experimental import pallas as pl
from jax.experimental.pallas import tpu as pltpu
from jax.sharding import PartitionSpec as P

STEP = 100
BF = jnp.bfloat16
F32 = jnp.float32


def swap(value, axis, bit, count):
    return lax.ppermute(value, axis, [(i, i ^ bit) for i in range(count)])


DEEP = 4


def partial_code_kernel(activations, basis, keep, send, act_buf, basis_buf, total, sems):
    feats = activations.shape[1]
    start = lax.axis_index("tensor") * feats
    step = feats // DEEP
    copies = []
    for k in range(DEEP):
        copies.append(
            pltpu.make_async_copy(
                basis.at[pl.ds(pl.multiple_of(start + k * step, step), step), :],
                basis_buf.at[k],
                sems.at[0, k],
            )
        )
        copies.append(
            pltpu.make_async_copy(
                activations.at[:, pl.ds(k * step, step)], act_buf.at[k], sems.at[1, k]
            )
        )
    for copy in copies:
        copy.start()
    for k in range(DEEP):
        copies[2 * k].wait()
        copies[2 * k + 1].wait()
        part = jnp.dot(act_buf[k], basis_buf[k], preferred_element_type=F32)
        total[...] = part if k == 0 else total[...] + part
    half = keep.shape[0]
    core = lax.rem(lax.axis_index("tensor"), 2)
    keep[...] = total[pl.ds(pl.multiple_of(core * half, half), half), :]
    send[...] = total[pl.ds(pl.multiple_of((1 - core) * half, half), half), :].astype(BF)


def partial_code(activations, basis):
    rows, feats = activations.shape
    rank = basis.shape[1]
    vmem = pl.BlockSpec(memory_space=pltpu.VMEM)
    hbm = pl.BlockSpec(memory_space=pltpu.HBM)
    return pl.pallas_call(
        partial_code_kernel,
        out_shape=(
            jax.ShapeDtypeStruct((rows // 2, rank), F32),
            jax.ShapeDtypeStruct((rows // 2, rank), BF),
        ),
        in_specs=[hbm, hbm],
        out_specs=(vmem, vmem),
        scratch_shapes=[
            pltpu.VMEM((DEEP, rows, feats // DEEP), BF),
            pltpu.VMEM((DEEP, feats // DEEP, rank), BF),
            pltpu.VMEM((rows, rank), F32),
            pltpu.SemaphoreType.DMA((2, DEEP)),
        ],
        compiler_params=pltpu.CompilerParams(vmem_limit_bytes=53 * 2**20),
        cost_estimate=pl.CostEstimate(
            flops=2 * rows * feats * rank,
            bytes_accessed=2 * feats * (rows + rank),
            transcendentals=0,
        ),
        name="partial_code",
    )(activations, basis)


def load_kernel(source, target, sems):
    count = DEEP if source.shape[0] % (16 * DEEP) == 0 else 1
    rows = source.shape[0] // count
    copies = [
        pltpu.make_async_copy(
            source.at[pl.ds(k * rows, rows), :], target.at[pl.ds(k * rows, rows), :], sems.at[k]
        )
        for k in range(count)
    ]
    for copy in copies:
        copy.start()
    for copy in copies:
        copy.wait()


def load(array):
    return pl.pallas_call(
        load_kernel,
        out_shape=jax.ShapeDtypeStruct(array.shape, array.dtype),
        in_specs=[pl.BlockSpec(memory_space=pltpu.HBM)],
        out_specs=pl.BlockSpec(memory_space=pltpu.VMEM),
        scratch_shapes=[pltpu.SemaphoreType.DMA((DEEP,))],
        compiler_params=pltpu.CompilerParams(vmem_limit_bytes=50 * 2**20),
        cost_estimate=pl.CostEstimate(
            flops=0, bytes_accessed=4 * array.size, transcendentals=0
        ),
        name="load",
    )(array)


def coded_total(keep, send, grad_rows, n_tensor):
    core = lax.axis_index("tensor") % 2
    total = keep + swap(send, "tensor", 1, n_tensor).astype(F32)
    bit = 2
    while bit < n_tensor:
        total_in = total.astype(BF)
        if bit == 2:
            total_in, grad_rows = lax.optimization_barrier((total_in, grad_rows))
            grad_rows = load(grad_rows)
        total = total + swap(total_in, "tensor", bit, n_tensor).astype(F32)
        total, grad_rows = lax.optimization_barrier((total, grad_rows))
        bit *= 2
    mine = total.astype(BF)
    theirs = swap(mine, "tensor", 1, n_tensor)
    coded = jnp.where(
        core == 0,
        jnp.concatenate([mine, theirs], 0),
        jnp.concatenate([theirs, mine], 0),
    )
    return coded, grad_rows


def line_total(grad_rows, coded, n_dp, cuts, spare=8):
    rows = grad_rows.shape[0] // n_dp
    d = lax.axis_index("dp")
    z, x = d // 2, d % 2
    first, second = cuts

    def both(block, code, cut):
        split = grad_rows.reshape(n_dp, rows, -1)
        part = lax.dynamic_slice_in_dim(split, block * 2, 2, 0)[:, cut[0] : cut[1]]
        return lax.dot_general(
            part, code, (((2,), (0,)), ((), ())), preferred_element_type=F32
        )

    def term(block, side, code, cut=(0, rows)):
        start = (block * 2 + side) * rows + cut[0]
        part = lax.dynamic_slice_in_dim(grad_rows, start, cut[1] - cut[0], 0)
        return jnp.dot(part, code, preferred_element_type=F32)

    def parity(value, side):
        return lax.dynamic_index_in_dim(value, side, 0, False).astype(F32)

    def hop(value, bit):
        full = [(i, i ^ (2 * bit)) for i in range(n_dp)]
        return lax.ppermute(value.astype(BF), "dp", full)

    def pair(value):
        return swap(value.astype(BF), "dp", 1, n_dp)

    def piece(value, cut):
        return value[cut[0] : cut[1]].astype(F32)

    def padded(value):
        return jnp.pad(value, ((0, rows - value.shape[0]), (0, 0)))

    got2 = pair(term(z ^ 2, 1 - x, coded))
    out1 = both(z ^ 1, coded, (0, first[1] + spare)).astype(BF)
    code, out1 = lax.optimization_barrier((coded, out1))
    near1 = hop(out1, 1)
    out3 = term(z ^ 3, 1 - x, code).astype(BF)
    got3 = pair(out3)

    sums = [(term(z ^ 2, x, coded, cut) + piece(got2, cut)).astype(BF) for cut in cuts]
    code, sums = lax.optimization_barrier((coded, sums))
    passed = [hop(part, 1) for part in sums]
    out1 = term(z ^ 1, 1 - x, code, second).astype(BF)
    code, out1, near1 = lax.optimization_barrier((code, out1, near1))
    got1 = pair(out1)
    near1 = near1[:, : first[1]]
    own_in = (term(z, 1 - x, code) + padded(parity(near1, 1 - x))).astype(BF)
    code, own_in = lax.optimization_barrier((coded, own_in))
    own = pair(own_in)
    def total(cut, part, code):
        value = term(z ^ 3, x, code, cut) + piece(got3, cut) + part.astype(F32)
        return lax.optimization_barrier((code, value.astype(BF)))

    code, total_a = total(first, passed[0], code)
    far_a = hop(total_a, 3)
    code, total_b = total(second, passed[1], code)
    far_b = hop(total_b, 3)
    late = hop(term(z ^ 1, x, code, second) + got1.astype(F32), 1)
    kept = [term(z, x, code, first) + parity(near1, x), term(z, x, code, second)]
    return kept, own, [(far_a,), (far_b, late)]


WIDE = 512


def adam_update_kernel(cut, n_terms, n_olds, own, got, first, second, basis, *refs):
    terms, refs = refs[:n_terms], refs[n_terms + n_olds :]
    new_first, new_second, update = refs[:3]
    first_buf, second_buf, direction, blocks, moment_sem, block_sem = refs[3:]
    here = pl.ds(cut[0], cut[1] - cut[0])
    grad = own[...] + got[here, :].astype(F32)
    for term in terms:
        grad = grad + term[...].astype(F32)
    first_buf[...] = 0.9 * first[here, :] + 0.1 * grad
    second_buf[...] = 0.999 * second[here, :] + 0.001 * grad * grad
    moments = [
        pltpu.make_async_copy(first_buf, new_first.at[here, :], moment_sem.at[0]),
        pltpu.make_async_copy(second_buf, new_second.at[here, :], moment_sem.at[1]),
    ]
    for copy in moments:
        copy.start()
    first_hat = first_buf[...] / (1.0 - 0.9**STEP)
    second_hat = second_buf[...] / (1.0 - 0.999**STEP)
    direction[...] = (first_hat / (jnp.sqrt(second_hat) + 1e-08)).astype(BF)

    def out_copy(j):
        return pltpu.make_async_copy(
            blocks.at[j], update.at[here, pl.ds(j * WIDE, WIDE)], block_sem.at[j]
        )

    count = basis.shape[0] // WIDE
    for j in range(count):
        part = lax.dot_general(
            direction[...],
            basis[pl.ds(j * WIDE, WIDE), :],
            (((1,), (1,)), ((), ())),
            preferred_element_type=F32,
        )
        blocks[j] = part.astype(BF)
        out_copy(j).start()
    for j in range(count):
        out_copy(j).wait()
    for copy in moments:
        copy.wait()


def adam_update(cut, own, got, terms, first, second, basis, olds):
    rows, rank = first.shape
    feats = basis.shape[0]
    here = cut[1] - cut[0]
    vmem = pl.BlockSpec(memory_space=pltpu.VMEM)
    hbm = pl.BlockSpec(memory_space=pl.ANY)
    n_inputs = 5 + len(terms)
    return pl.pallas_call(
        functools.partial(adam_update_kernel, cut, len(terms), len(olds)),
        out_shape=(
            jax.ShapeDtypeStruct((rows, rank), F32),
            jax.ShapeDtypeStruct((rows, rank), F32),
            jax.ShapeDtypeStruct((rows, feats), BF),
        ),
        in_specs=[vmem] * n_inputs + [hbm] * len(olds),
        out_specs=(hbm, hbm, hbm),
        input_output_aliases={n_inputs + i: i for i in range(len(olds))},
        scratch_shapes=[
            pltpu.VMEM((here, rank), F32),
            pltpu.VMEM((here, rank), F32),
            pltpu.VMEM((here, rank), BF),
            pltpu.VMEM((feats // WIDE, here, WIDE), BF),
            pltpu.SemaphoreType.DMA((2,)),
            pltpu.SemaphoreType.DMA((feats // WIDE,)),
        ],
        compiler_params=pltpu.CompilerParams(vmem_limit_bytes=24 * 2**20),
        cost_estimate=pl.CostEstimate(
            flops=2 * here * rank * feats,
            bytes_accessed=2 * here * feats + 2 * rank * feats,
            transcendentals=here * rank,
        ),
        name="adam_update",
    )(own, got, first, second, basis, *terms, *olds)


def on_device(activations, basis, out_grad, first_moment, second_moment):
    n_tensor = lax.axis_size("tensor")
    n_dp = lax.axis_size("dp")
    keep, send = partial_code(activations, basis)
    coded_rows, grad_rows = coded_total(keep, send, out_grad.T, n_tensor)
    if n_dp == 8:
        rows = first_moment.shape[1]
        middle = rows // 32 * 16
        cuts = ((0, middle), (middle, rows))
        kept, got, fars = line_total(grad_rows, coded_rows, n_dp, cuts)
        outs = ()
        for cut, own, terms in zip(cuts, kept, fars):
            outs = adam_update(
                cut, own, got, terms, first_moment[0], second_moment[0], basis, outs
            )
        return tuple(out[None] for out in outs)
    term = jnp.dot(grad_rows, coded_rows, preferred_element_type=F32)
    coded_grad = lax.psum_scatter(term, "dp", scatter_dimension=0, tiled=True)[None]
    new_first = 0.9 * first_moment + 0.1 * coded_grad
    new_second = 0.999 * second_moment + 0.001 * coded_grad * coded_grad
    first_hat = new_first / (1.0 - 0.9**STEP)
    second_hat = new_second / (1.0 - 0.999**STEP)
    direction = (first_hat / (jnp.sqrt(second_hat) + 1e-08)).astype(BF)
    update = lax.dot_general(
        direction[0], basis, (((1,), (1,)), ((), ())), preferred_element_type=F32
    )
    return (new_first, new_second, update.astype(BF)[None])


def solution(mesh):
    placed = (
        P("dp", "tensor"),
        P(),
        P("dp", "tensor"),
        P("tensor", "dp", None),
        P("tensor", "dp", None),
    )
    return jax.shard_map(
        on_device,
        mesh=mesh,
        in_specs=placed,
        out_specs=(P("tensor", "dp", None), P("tensor", "dp", None), P("tensor", "dp", None)),
        check_vma=False,
    )
```

```python
import functools

import jax
import jax.numpy as jnp
from jax import lax
from jax.experimental import pallas as pl
from jax.experimental.pallas import tpu as pltpu
from jax.sharding import PartitionSpec as P

STEP = 100
BF = jnp.bfloat16
F32 = jnp.float32


def swap(value, axis, bit, count):
    return lax.ppermute(value, axis, [(i, i ^ bit) for i in range(count)])


DEEP = 4


def partial_code_kernel(activations, basis, keep, send, act_buf, basis_buf, total, sems):
    feats = activations.shape[1]
    start = lax.axis_index("tensor") * feats
    step = feats // DEEP
    copies = []
    for k in range(DEEP):
        copies.append(
            pltpu.make_async_copy(
                basis.at[pl.ds(pl.multiple_of(start + k * step, step), step), :],
                basis_buf.at[k],
                sems.at[0, k],
            )
        )
        copies.append(
            pltpu.make_async_copy(
                activations.at[:, pl.ds(k * step, step)], act_buf.at[k], sems.at[1, k]
            )
        )
    for copy in copies:
        copy.start()
    for k in range(DEEP):
        copies[2 * k].wait()
        copies[2 * k + 1].wait()
        part = jnp.dot(act_buf[k], basis_buf[k], preferred_element_type=F32)
        total[...] = part if k == 0 else total[...] + part
    half = keep.shape[0]
    core = lax.rem(lax.axis_index("tensor"), 2)
    keep[...] = total[pl.ds(pl.multiple_of(core * half, half), half), :]
    send[...] = total[pl.ds(pl.multiple_of((1 - core) * half, half), half), :].astype(BF)


def partial_code(activations, basis):
    rows, feats = activations.shape
    rank = basis.shape[1]
    vmem = pl.BlockSpec(memory_space=pltpu.VMEM)
    hbm = pl.BlockSpec(memory_space=pltpu.HBM)
    return pl.pallas_call(
        partial_code_kernel,
        out_shape=(
            jax.ShapeDtypeStruct((rows // 2, rank), F32),
            jax.ShapeDtypeStruct((rows // 2, rank), BF),
        ),
        in_specs=[hbm, hbm],
        out_specs=(vmem, vmem),
        scratch_shapes=[
            pltpu.VMEM((DEEP, rows, feats // DEEP), BF),
            pltpu.VMEM((DEEP, feats // DEEP, rank), BF),
            pltpu.VMEM((rows, rank), F32),
            pltpu.SemaphoreType.DMA((2, DEEP)),
        ],
        compiler_params=pltpu.CompilerParams(vmem_limit_bytes=53 * 2**20),
        cost_estimate=pl.CostEstimate(
            flops=2 * rows * feats * rank,
            bytes_accessed=2 * feats * (rows + rank),
            transcendentals=0,
        ),
        name="partial_code",
    )(activations, basis)


def coded_total(keep, send, n_tensor):
    core = lax.axis_index("tensor") % 2
    total = keep + swap(send, "tensor", 1, n_tensor).astype(F32)
    bit = 2
    while bit < n_tensor:
        total = total + swap(total.astype(BF), "tensor", bit, n_tensor).astype(F32)
        bit *= 2
    mine = total.astype(BF)
    theirs = swap(mine, "tensor", 1, n_tensor)
    return jnp.where(
        core == 0,
        jnp.concatenate([mine, theirs], 0),
        jnp.concatenate([theirs, mine], 0),
    )


def line_total(grad_rows, coded, n_dp, cuts, spare=8):
    rows = grad_rows.shape[0] // n_dp
    d = lax.axis_index("dp")
    z, x = d // 2, d % 2
    first, second = cuts

    def both(block, code, cut):
        split = grad_rows.reshape(n_dp, rows, -1)
        part = lax.dynamic_slice_in_dim(split, block * 2, 2, 0)[:, cut[0] : cut[1]]
        return lax.dot_general(
            part, code, (((2,), (0,)), ((), ())), preferred_element_type=F32
        )

    def term(block, side, code, cut=(0, rows)):
        start = (block * 2 + side) * rows + cut[0]
        part = lax.dynamic_slice_in_dim(grad_rows, start, cut[1] - cut[0], 0)
        return jnp.dot(part, code, preferred_element_type=F32)

    def parity(value, side):
        return lax.dynamic_index_in_dim(value, side, 0, False).astype(F32)

    def hop(value, bit):
        full = [(i, i ^ (2 * bit)) for i in range(n_dp)]
        return lax.ppermute(value.astype(BF), "dp", full)

    def pair(value):
        return swap(value.astype(BF), "dp", 1, n_dp)

    def piece(value, cut):
        return value[cut[0] : cut[1]].astype(F32)

    def padded(value):
        return jnp.pad(value, ((0, rows - value.shape[0]), (0, 0)))

    got2 = pair(term(z ^ 2, 1 - x, coded))
    out1 = both(z ^ 1, coded, (0, first[1] + spare)).astype(BF)
    code, out1 = lax.optimization_barrier((coded, out1))
    near1 = hop(out1, 1)
    n_first = first[1]
    got31 = jnp.concatenate(
        [term(z ^ 3, 1 - x, code, first), term(z ^ 1, 1 - x, code, second)]
    )
    got31 = pair(got31)

    sums = [(term(z ^ 2, x, coded, cut) + piece(got2, cut)).astype(BF) for cut in cuts]
    code, sums = lax.optimization_barrier((coded, sums))
    passed = [hop(part, 1) for part in sums]
    out3 = term(z ^ 3, 1 - x, code, second).astype(BF)
    code, out3, near1 = lax.optimization_barrier((code, out3, near1))
    got3 = pair(out3)
    near1 = near1[:, : first[1]]
    own_in = (term(z, 1 - x, code) + padded(parity(near1, 1 - x))).astype(BF)
    code, own_in = lax.optimization_barrier((coded, own_in))
    own = pair(own_in)

    def total(block, cut, code, *parts):
        value = term(block, x, code, cut)
        for part in parts:
            value = value + part.astype(F32)
        return lax.optimization_barrier((code, value.astype(BF)))

    code, total_a = total(z ^ 3, first, code, got31[:n_first], passed[0])
    far_a = hop(total_a, 3)
    code, late = total(z ^ 1, second, code, got31[n_first:])
    late = hop(late, 1)
    code, total_b = total(z ^ 3, second, code, got3, passed[1])
    far_b = hop(total_b, 3)
    kept = [term(z, x, code, first) + parity(near1, x), term(z, x, code, second)]
    return kept, own, [(far_a,), (late, far_b)]


WIDE = 512


def adam_update_kernel(cut, n_terms, n_olds, own, got, first, second, basis, *refs):
    terms, refs = refs[:n_terms], refs[n_terms + n_olds :]
    new_first, new_second, update = refs[:3]
    first_buf, second_buf, direction, blocks, moment_sem, block_sem = refs[3:]
    here = pl.ds(cut[0], cut[1] - cut[0])
    grad = own[...] + got[here, :].astype(F32)
    for term in terms:
        grad = grad + term[...].astype(F32)
    first_buf[...] = 0.9 * first[here, :] + 0.1 * grad
    second_buf[...] = 0.999 * second[here, :] + 0.001 * grad * grad
    moments = [
        pltpu.make_async_copy(first_buf, new_first.at[here, :], moment_sem.at[0]),
        pltpu.make_async_copy(second_buf, new_second.at[here, :], moment_sem.at[1]),
    ]
    for copy in moments:
        copy.start()
    first_hat = first_buf[...] / (1.0 - 0.9**STEP)
    second_hat = second_buf[...] / (1.0 - 0.999**STEP)
    direction[...] = (first_hat / (jnp.sqrt(second_hat) + 1e-08)).astype(BF)

    def out_copy(j):
        return pltpu.make_async_copy(
            blocks.at[j], update.at[here, pl.ds(j * WIDE, WIDE)], block_sem.at[j]
        )

    count = basis.shape[0] // WIDE
    for j in range(count):
        part = lax.dot_general(
            direction[...],
            basis[pl.ds(j * WIDE, WIDE), :],
            (((1,), (1,)), ((), ())),
            preferred_element_type=F32,
        )
        blocks[j] = part.astype(BF)
        out_copy(j).start()
    for j in range(count):
        out_copy(j).wait()
    for copy in moments:
        copy.wait()


def adam_update(cut, own, got, terms, first, second, basis, olds):
    rows, rank = first.shape
    feats = basis.shape[0]
    here = cut[1] - cut[0]
    vmem = pl.BlockSpec(memory_space=pltpu.VMEM)
    hbm = pl.BlockSpec(memory_space=pl.ANY)
    n_inputs = 5 + len(terms)
    return pl.pallas_call(
        functools.partial(adam_update_kernel, cut, len(terms), len(olds)),
        out_shape=(
            jax.ShapeDtypeStruct((rows, rank), F32),
            jax.ShapeDtypeStruct((rows, rank), F32),
            jax.ShapeDtypeStruct((rows, feats), BF),
        ),
        in_specs=[vmem] * n_inputs + [hbm] * len(olds),
        out_specs=(hbm, hbm, hbm),
        input_output_aliases={n_inputs + i: i for i in range(len(olds))},
        scratch_shapes=[
            pltpu.VMEM((here, rank), F32),
            pltpu.VMEM((here, rank), F32),
            pltpu.VMEM((here, rank), BF),
            pltpu.VMEM((feats // WIDE, here, WIDE), BF),
            pltpu.SemaphoreType.DMA((2,)),
            pltpu.SemaphoreType.DMA((feats // WIDE,)),
        ],
        compiler_params=pltpu.CompilerParams(vmem_limit_bytes=24 * 2**20),
        cost_estimate=pl.CostEstimate(
            flops=2 * here * rank * feats,
            bytes_accessed=2 * here * feats + 2 * rank * feats,
            transcendentals=here * rank,
        ),
        name="adam_update",
    )(own, got, first, second, basis, *terms, *olds)


def on_device(activations, basis, out_grad, first_moment, second_moment):
    n_tensor = lax.axis_size("tensor")
    n_dp = lax.axis_size("dp")
    keep, send = partial_code(activations, basis)
    coded_rows = coded_total(keep, send, n_tensor)
    if n_dp == 8:
        rows = first_moment.shape[1]
        middle = rows // 32 * 16
        cuts = ((0, middle), (middle, rows))
        kept, got, fars = line_total(out_grad.T, coded_rows, n_dp, cuts)
        outs = ()
        for cut, own, terms in zip(cuts, kept, fars):
            outs = adam_update(
                cut, own, got, terms, first_moment[0], second_moment[0], basis, outs
            )
        return tuple(out[None] for out in outs)
    term = jnp.dot(out_grad.T, coded_rows, preferred_element_type=F32)
    coded_grad = lax.psum_scatter(term, "dp", scatter_dimension=0, tiled=True)[None]
    new_first = 0.9 * first_moment + 0.1 * coded_grad
    new_second = 0.999 * second_moment + 0.001 * coded_grad * coded_grad
    first_hat = new_first / (1.0 - 0.9**STEP)
    second_hat = new_second / (1.0 - 0.999**STEP)
    direction = (first_hat / (jnp.sqrt(second_hat) + 1e-08)).astype(BF)
    update = lax.dot_general(
        direction[0], basis, (((1,), (1,)), ((), ())), preferred_element_type=F32
    )
    return (new_first, new_second, update.astype(BF)[None])


def solution(mesh):
    placed = (
        P("dp", "tensor"),
        P(),
        P("dp", "tensor"),
        P("tensor", "dp", None),
        P("tensor", "dp", None),
    )
    return jax.shard_map(
        on_device,
        mesh=mesh,
        in_specs=placed,
        out_specs=(P("tensor", "dp", None), P("tensor", "dp", None), P("tensor", "dp", None)),
        check_vma=False,
    )
```

```python
import functools

import jax
import jax.numpy as jnp
from jax import lax
from jax.experimental import pallas as pl
from jax.experimental.pallas import tpu as pltpu
from jax.sharding import PartitionSpec as P

STEP = 100
BF = jnp.bfloat16
F32 = jnp.float32


def swap(value, axis, bit, count):
    return lax.ppermute(value, axis, [(i, i ^ bit) for i in range(count)])


DEEP = 4


def partial_code_kernel(activations, basis, keep, send, act_buf, basis_buf, total, sems):
    feats = activations.shape[1]
    start = lax.axis_index("tensor") * feats
    step = feats // DEEP
    copies = []
    for k in range(DEEP):
        copies.append(
            pltpu.make_async_copy(
                basis.at[pl.ds(pl.multiple_of(start + k * step, step), step), :],
                basis_buf.at[k],
                sems.at[0, k],
            )
        )
        copies.append(
            pltpu.make_async_copy(
                activations.at[:, pl.ds(k * step, step)], act_buf.at[k], sems.at[1, k]
            )
        )
    for copy in copies:
        copy.start()
    for k in range(DEEP):
        copies[2 * k].wait()
        copies[2 * k + 1].wait()
        part = jnp.dot(act_buf[k], basis_buf[k], preferred_element_type=F32)
        total[...] = part if k == 0 else total[...] + part
    half = keep.shape[0]
    core = lax.rem(lax.axis_index("tensor"), 2)
    keep[...] = total[pl.ds(pl.multiple_of(core * half, half), half), :]
    send[...] = total[pl.ds(pl.multiple_of((1 - core) * half, half), half), :].astype(BF)


def partial_code(activations, basis):
    rows, feats = activations.shape
    rank = basis.shape[1]
    vmem = pl.BlockSpec(memory_space=pltpu.VMEM)
    hbm = pl.BlockSpec(memory_space=pltpu.HBM)
    return pl.pallas_call(
        partial_code_kernel,
        out_shape=(
            jax.ShapeDtypeStruct((rows // 2, rank), F32),
            jax.ShapeDtypeStruct((rows // 2, rank), BF),
        ),
        in_specs=[hbm, hbm],
        out_specs=(vmem, vmem),
        scratch_shapes=[
            pltpu.VMEM((DEEP, rows, feats // DEEP), BF),
            pltpu.VMEM((DEEP, feats // DEEP, rank), BF),
            pltpu.VMEM((rows, rank), F32),
            pltpu.SemaphoreType.DMA((2, DEEP)),
        ],
        compiler_params=pltpu.CompilerParams(vmem_limit_bytes=53 * 2**20),
        cost_estimate=pl.CostEstimate(
            flops=2 * rows * feats * rank,
            bytes_accessed=2 * feats * (rows + rank),
            transcendentals=0,
        ),
        name="partial_code",
    )(activations, basis)


def coded_total(keep, send, n_tensor):
    core = lax.axis_index("tensor") % 2
    total = keep + swap(send, "tensor", 1, n_tensor).astype(F32)
    bit = 2
    while bit < n_tensor:
        total = total + swap(total.astype(BF), "tensor", bit, n_tensor).astype(F32)
        bit *= 2
    mine = total.astype(BF)
    theirs = swap(mine, "tensor", 1, n_tensor)
    return jnp.where(
        core == 0,
        jnp.concatenate([mine, theirs], 0),
        jnp.concatenate([theirs, mine], 0),
    )


def line_total(grad_rows, coded, n_dp, cuts, spare=8):
    rows = grad_rows.shape[0] // n_dp
    d = lax.axis_index("dp")
    z, x = d // 2, d % 2
    first, second = cuts

    def both(block, code, cut):
        split = grad_rows.reshape(n_dp, rows, -1)
        part = lax.dynamic_slice_in_dim(split, block * 2, 2, 0)[:, cut[0] : cut[1]]
        return lax.dot_general(
            part, code, (((2,), (0,)), ((), ())), preferred_element_type=F32
        )

    def term(block, side, code, cut=(0, rows)):
        start = (block * 2 + side) * rows + cut[0]
        part = lax.dynamic_slice_in_dim(grad_rows, start, cut[1] - cut[0], 0)
        return jnp.dot(part, code, preferred_element_type=F32)

    def parity(value, side):
        return lax.dynamic_index_in_dim(value, side, 0, False).astype(F32)

    def hop(value, bit):
        full = [(i, i ^ (2 * bit)) for i in range(n_dp)]
        return lax.ppermute(value.astype(BF), "dp", full)

    def pair(value):
        return swap(value.astype(BF), "dp", 1, n_dp)

    def piece(value, cut):
        return value[cut[0] : cut[1]].astype(F32)

    def padded(value):
        return jnp.pad(value, ((0, rows - value.shape[0]), (0, 0)))

    got2 = pair(term(z ^ 2, 1 - x, coded))
    out1 = both(z ^ 1, coded, (0, first[1] + spare)).astype(BF)
    code, out1 = lax.optimization_barrier((coded, out1))
    near1 = hop(out1, 1)
    n_first = first[1]
    got31 = jnp.concatenate(
        [term(z ^ 3, 1 - x, code, first), term(z ^ 1, 1 - x, code, second)]
    )
    got31 = pair(got31)

    def near_sum(cut, code):
        value = (term(z ^ 2, x, code, cut) + piece(got2, cut)).astype(BF)
        return lax.optimization_barrier((code, value))

    code, sum_a = near_sum(first, coded)
    passed = [hop(sum_a, 1)]
    out3 = term(z ^ 3, 1 - x, code, second).astype(BF)
    code, out3, near1 = lax.optimization_barrier((code, out3, near1))
    code, sum_b = near_sum(second, code)
    passed.append(hop(sum_b, 1))
    got3 = pair(out3)
    near1 = near1[:, : first[1]]
    own_in = (term(z, 1 - x, code) + padded(parity(near1, 1 - x))).astype(BF)
    code, own_in = lax.optimization_barrier((coded, own_in))
    own = pair(own_in)

    def total(block, cut, code, *parts):
        value = term(block, x, code, cut)
        for part in parts:
            value = value + part.astype(F32)
        return lax.optimization_barrier((code, value.astype(BF)))

    code, total_a = total(z ^ 3, first, code, got31[:n_first], passed[0])
    far_a = hop(total_a, 3)
    code, late = total(z ^ 1, second, code, got31[n_first:])
    late = hop(late, 1)
    code, total_b = total(z ^ 3, second, code, got3, passed[1])
    far_b = hop(total_b, 3)
    kept = [term(z, x, code, first) + parity(near1, x), term(z, x, code, second)]
    return kept, own, [(far_a,), (late, far_b)]


WIDE = 512


def adam_update_kernel(cut, n_terms, n_olds, own, got, first, second, basis, *refs):
    terms, refs = refs[:n_terms], refs[n_terms + n_olds :]
    new_first, new_second, update = refs[:3]
    first_buf, second_buf, direction, blocks, moment_sem, block_sem = refs[3:]
    here = pl.ds(cut[0], cut[1] - cut[0])
    grad = own[...] + got[here, :].astype(F32)
    for term in terms:
        grad = grad + term[...].astype(F32)
    first_buf[...] = 0.9 * first[here, :] + 0.1 * grad
    second_buf[...] = 0.999 * second[here, :] + 0.001 * grad * grad
    moments = [
        pltpu.make_async_copy(first_buf, new_first.at[here, :], moment_sem.at[0]),
        pltpu.make_async_copy(second_buf, new_second.at[here, :], moment_sem.at[1]),
    ]
    for copy in moments:
        copy.start()
    first_hat = first_buf[...] / (1.0 - 0.9**STEP)
    second_hat = second_buf[...] / (1.0 - 0.999**STEP)
    direction[...] = (first_hat / (jnp.sqrt(second_hat) + 1e-08)).astype(BF)

    def out_copy(j):
        return pltpu.make_async_copy(
            blocks.at[j], update.at[here, pl.ds(j * WIDE, WIDE)], block_sem.at[j]
        )

    count = basis.shape[0] // WIDE
    for j in range(count):
        part = lax.dot_general(
            direction[...],
            basis[pl.ds(j * WIDE, WIDE), :],
            (((1,), (1,)), ((), ())),
            preferred_element_type=F32,
        )
        blocks[j] = part.astype(BF)
        out_copy(j).start()
    for j in range(count):
        out_copy(j).wait()
    for copy in moments:
        copy.wait()


def adam_update(cut, own, got, terms, first, second, basis, olds):
    rows, rank = first.shape
    feats = basis.shape[0]
    here = cut[1] - cut[0]
    vmem = pl.BlockSpec(memory_space=pltpu.VMEM)
    hbm = pl.BlockSpec(memory_space=pl.ANY)
    n_inputs = 5 + len(terms)
    return pl.pallas_call(
        functools.partial(adam_update_kernel, cut, len(terms), len(olds)),
        out_shape=(
            jax.ShapeDtypeStruct((rows, rank), F32),
            jax.ShapeDtypeStruct((rows, rank), F32),
            jax.ShapeDtypeStruct((rows, feats), BF),
        ),
        in_specs=[vmem] * n_inputs + [hbm] * len(olds),
        out_specs=(hbm, hbm, hbm),
        input_output_aliases={n_inputs + i: i for i in range(len(olds))},
        scratch_shapes=[
            pltpu.VMEM((here, rank), F32),
            pltpu.VMEM((here, rank), F32),
            pltpu.VMEM((here, rank), BF),
            pltpu.VMEM((feats // WIDE, here, WIDE), BF),
            pltpu.SemaphoreType.DMA((2,)),
            pltpu.SemaphoreType.DMA((feats // WIDE,)),
        ],
        compiler_params=pltpu.CompilerParams(vmem_limit_bytes=24 * 2**20),
        cost_estimate=pl.CostEstimate(
            flops=2 * here * rank * feats,
            bytes_accessed=2 * here * feats + 2 * rank * feats,
            transcendentals=here * rank,
        ),
        name="adam_update",
    )(own, got, first, second, basis, *terms, *olds)


def on_device(activations, basis, out_grad, first_moment, second_moment):
    n_tensor = lax.axis_size("tensor")
    n_dp = lax.axis_size("dp")
    keep, send = partial_code(activations, basis)
    coded_rows = coded_total(keep, send, n_tensor)
    if n_dp == 8:
        rows = first_moment.shape[1]
        middle = rows // 32 * 16
        cuts = ((0, middle), (middle, rows))
        kept, got, fars = line_total(out_grad.T, coded_rows, n_dp, cuts)
        outs = ()
        for cut, own, terms in zip(cuts, kept, fars):
            outs = adam_update(
                cut, own, got, terms, first_moment[0], second_moment[0], basis, outs
            )
        return tuple(out[None] for out in outs)
    term = jnp.dot(out_grad.T, coded_rows, preferred_element_type=F32)
    coded_grad = lax.psum_scatter(term, "dp", scatter_dimension=0, tiled=True)[None]
    new_first = 0.9 * first_moment + 0.1 * coded_grad
    new_second = 0.999 * second_moment + 0.001 * coded_grad * coded_grad
    first_hat = new_first / (1.0 - 0.9**STEP)
    second_hat = new_second / (1.0 - 0.999**STEP)
    direction = (first_hat / (jnp.sqrt(second_hat) + 1e-08)).astype(BF)
    update = lax.dot_general(
        direction[0], basis, (((1,), (1,)), ((), ())), preferred_element_type=F32
    )
    return (new_first, new_second, update.astype(BF)[None])


def solution(mesh):
    placed = (
        P("dp", "tensor"),
        P(),
        P("dp", "tensor"),
        P("tensor", "dp", None),
        P("tensor", "dp", None),
    )
    return jax.shard_map(
        on_device,
        mesh=mesh,
        in_specs=placed,
        out_specs=(P("tensor", "dp", None), P("tensor", "dp", None), P("tensor", "dp", None)),
        check_vma=False,
    )
```

```python
import functools

import jax
import jax.numpy as jnp
from jax import lax
from jax.experimental import pallas as pl
from jax.experimental.pallas import tpu as pltpu
from jax.sharding import PartitionSpec as P

STEP = 100
BF = jnp.bfloat16
F32 = jnp.float32


def swap(value, axis, bit, count):
    return lax.ppermute(value, axis, [(i, i ^ bit) for i in range(count)])


DEEP = 4


def partial_code_kernel(activations, basis, keep, send, act_buf, basis_buf, total, sems):
    feats = activations.shape[1]
    start = lax.axis_index("tensor") * feats
    step = feats // DEEP
    copies = []
    for k in range(DEEP):
        copies.append(
            pltpu.make_async_copy(
                basis.at[pl.ds(pl.multiple_of(start + k * step, step), step), :],
                basis_buf.at[k],
                sems.at[0, k],
            )
        )
        copies.append(
            pltpu.make_async_copy(
                activations.at[:, pl.ds(k * step, step)], act_buf.at[k], sems.at[1, k]
            )
        )
    for copy in copies:
        copy.start()
    for k in range(DEEP):
        copies[2 * k].wait()
        copies[2 * k + 1].wait()
        part = jnp.dot(act_buf[k], basis_buf[k], preferred_element_type=F32)
        total[...] = part if k == 0 else total[...] + part
    half = keep.shape[0]
    core = lax.rem(lax.axis_index("tensor"), 2)
    keep[...] = total[pl.ds(pl.multiple_of(core * half, half), half), :]
    send[...] = total[pl.ds(pl.multiple_of((1 - core) * half, half), half), :].astype(BF)


def partial_code(activations, basis):
    rows, feats = activations.shape
    rank = basis.shape[1]
    vmem = pl.BlockSpec(memory_space=pltpu.VMEM)
    hbm = pl.BlockSpec(memory_space=pltpu.HBM)
    return pl.pallas_call(
        partial_code_kernel,
        out_shape=(
            jax.ShapeDtypeStruct((rows // 2, rank), F32),
            jax.ShapeDtypeStruct((rows // 2, rank), BF),
        ),
        in_specs=[hbm, hbm],
        out_specs=(vmem, vmem),
        scratch_shapes=[
            pltpu.VMEM((DEEP, rows, feats // DEEP), BF),
            pltpu.VMEM((DEEP, feats // DEEP, rank), BF),
            pltpu.VMEM((rows, rank), F32),
            pltpu.SemaphoreType.DMA((2, DEEP)),
        ],
        compiler_params=pltpu.CompilerParams(vmem_limit_bytes=53 * 2**20),
        cost_estimate=pl.CostEstimate(
            flops=2 * rows * feats * rank,
            bytes_accessed=2 * feats * (rows + rank),
            transcendentals=0,
        ),
        name="partial_code",
    )(activations, basis)


def coded_total(keep, send, n_tensor):
    core = lax.axis_index("tensor") % 2
    total = keep + swap(send, "tensor", 1, n_tensor).astype(F32)
    bit = 2
    while bit < n_tensor:
        total = total + swap(total.astype(BF), "tensor", bit, n_tensor).astype(F32)
        bit *= 2
    mine = total.astype(BF)
    theirs = swap(mine, "tensor", 1, n_tensor)
    return jnp.where(
        core == 0,
        jnp.concatenate([mine, theirs], 0),
        jnp.concatenate([theirs, mine], 0),
    )


def line_total(grad_rows, coded, n_dp, cuts, spare=8):
    rows = grad_rows.shape[0] // n_dp
    d = lax.axis_index("dp")
    z, x = d // 2, d % 2
    first, second = cuts

    def both(block, code, cut):
        split = grad_rows.reshape(n_dp, rows, -1)
        part = lax.dynamic_slice_in_dim(split, block * 2, 2, 0)[:, cut[0] : cut[1]]
        return lax.dot_general(
            part, code, (((2,), (0,)), ((), ())), preferred_element_type=F32
        )

    def term(block, side, code, cut=(0, rows)):
        start = (block * 2 + side) * rows + cut[0]
        part = lax.dynamic_slice_in_dim(grad_rows, start, cut[1] - cut[0], 0)
        return jnp.dot(part, code, preferred_element_type=F32)

    def parity(value, side):
        return lax.dynamic_index_in_dim(value, side, 0, False).astype(F32)

    def hop(value, bit):
        full = [(i, i ^ (2 * bit)) for i in range(n_dp)]
        return lax.ppermute(value.astype(BF), "dp", full)

    def pair(value):
        return swap(value.astype(BF), "dp", 1, n_dp)

    def piece(value, cut):
        return value[cut[0] : cut[1]].astype(F32)

    def padded(value):
        return jnp.pad(value, ((0, rows - value.shape[0]), (0, 0)))

    got2 = pair(term(z ^ 2, 1 - x, coded))
    out1 = both(z ^ 1, coded, (0, first[1] + spare)).astype(BF)
    code, out1 = lax.optimization_barrier((coded, out1))
    near1 = hop(out1, 1)
    n_first = first[1]
    got31 = jnp.concatenate(
        [term(z ^ 3, 1 - x, code, first), term(z ^ 1, 1 - x, code, second)]
    )
    got31 = pair(got31)

    sums = [(term(z ^ 2, x, coded, cut) + piece(got2, cut)).astype(BF) for cut in cuts]
    code, sums = lax.optimization_barrier((coded, sums))
    passed = [hop(part, 1) for part in sums]
    out3 = term(z ^ 3, 1 - x, code, second).astype(BF)
    code, out3, near1 = lax.optimization_barrier((code, out3, near1))
    got3 = pair(out3)
    near1 = near1[:, : first[1]]
    own_in = (term(z, 1 - x, code) + padded(parity(near1, 1 - x))).astype(BF)
    code, own_in = lax.optimization_barrier((coded, own_in))
    own = pair(own_in)

    def total(block, cut, code, *parts):
        value = term(block, x, code, cut)
        for part in parts:
            value = value + part.astype(F32)
        return lax.optimization_barrier((code, value.astype(BF)))

    code, total_a = total(z ^ 3, first, code, got31[:n_first], passed[0])
    far_a = hop(total_a, 3)
    code, got31, passed[1] = lax.optimization_barrier((code, got31, passed[1]))
    code, late = total(z ^ 1, second, code, got31[n_first:])
    late = hop(late, 1)
    code, total_b = total(z ^ 3, second, code, got3, passed[1])
    far_b = hop(total_b, 3)
    kept = [term(z, x, code, first) + parity(near1, x), term(z, x, code, second)]
    return kept, own, [(far_a,), (late, far_b)]


WIDE = 512


def adam_update_kernel(cut, n_terms, n_olds, own, got, first, second, basis, *refs):
    terms, refs = refs[:n_terms], refs[n_terms + n_olds :]
    new_first, new_second, update = refs[:3]
    first_buf, second_buf, direction, blocks, moment_sem, block_sem = refs[3:]
    here = pl.ds(cut[0], cut[1] - cut[0])
    grad = own[...] + got[here, :].astype(F32)
    for term in terms:
        grad = grad + term[...].astype(F32)
    first_buf[...] = 0.9 * first[here, :] + 0.1 * grad
    second_buf[...] = 0.999 * second[here, :] + 0.001 * grad * grad
    moments = [
        pltpu.make_async_copy(first_buf, new_first.at[here, :], moment_sem.at[0]),
        pltpu.make_async_copy(second_buf, new_second.at[here, :], moment_sem.at[1]),
    ]
    for copy in moments:
        copy.start()
    first_hat = first_buf[...] / (1.0 - 0.9**STEP)
    second_hat = second_buf[...] / (1.0 - 0.999**STEP)
    direction[...] = (first_hat / (jnp.sqrt(second_hat) + 1e-08)).astype(BF)

    def out_copy(j):
        return pltpu.make_async_copy(
            blocks.at[j], update.at[here, pl.ds(j * WIDE, WIDE)], block_sem.at[j]
        )

    count = basis.shape[0] // WIDE
    for j in range(count):
        part = lax.dot_general(
            direction[...],
            basis[pl.ds(j * WIDE, WIDE), :],
            (((1,), (1,)), ((), ())),
            preferred_element_type=F32,
        )
        blocks[j] = part.astype(BF)
        out_copy(j).start()
    for j in range(count):
        out_copy(j).wait()
    for copy in moments:
        copy.wait()


def adam_update(cut, own, got, terms, first, second, basis, olds):
    rows, rank = first.shape
    feats = basis.shape[0]
    here = cut[1] - cut[0]
    vmem = pl.BlockSpec(memory_space=pltpu.VMEM)
    hbm = pl.BlockSpec(memory_space=pl.ANY)
    n_inputs = 5 + len(terms)
    return pl.pallas_call(
        functools.partial(adam_update_kernel, cut, len(terms), len(olds)),
        out_shape=(
            jax.ShapeDtypeStruct((rows, rank), F32),
            jax.ShapeDtypeStruct((rows, rank), F32),
            jax.ShapeDtypeStruct((rows, feats), BF),
        ),
        in_specs=[vmem] * n_inputs + [hbm] * len(olds),
        out_specs=(hbm, hbm, hbm),
        input_output_aliases={n_inputs + i: i for i in range(len(olds))},
        scratch_shapes=[
            pltpu.VMEM((here, rank), F32),
            pltpu.VMEM((here, rank), F32),
            pltpu.VMEM((here, rank), BF),
            pltpu.VMEM((feats // WIDE, here, WIDE), BF),
            pltpu.SemaphoreType.DMA((2,)),
            pltpu.SemaphoreType.DMA((feats // WIDE,)),
        ],
        compiler_params=pltpu.CompilerParams(vmem_limit_bytes=24 * 2**20),
        cost_estimate=pl.CostEstimate(
            flops=2 * here * rank * feats,
            bytes_accessed=2 * here * feats + 2 * rank * feats,
            transcendentals=here * rank,
        ),
        name="adam_update",
    )(own, got, first, second, basis, *terms, *olds)


def on_device(activations, basis, out_grad, first_moment, second_moment):
    n_tensor = lax.axis_size("tensor")
    n_dp = lax.axis_size("dp")
    keep, send = partial_code(activations, basis)
    coded_rows = coded_total(keep, send, n_tensor)
    if n_dp == 8:
        rows = first_moment.shape[1]
        middle = rows // 32 * 16
        cuts = ((0, middle), (middle, rows))
        kept, got, fars = line_total(out_grad.T, coded_rows, n_dp, cuts)
        outs = ()
        for cut, own, terms in zip(cuts, kept, fars):
            outs = adam_update(
                cut, own, got, terms, first_moment[0], second_moment[0], basis, outs
            )
        return tuple(out[None] for out in outs)
    term = jnp.dot(out_grad.T, coded_rows, preferred_element_type=F32)
    coded_grad = lax.psum_scatter(term, "dp", scatter_dimension=0, tiled=True)[None]
    new_first = 0.9 * first_moment + 0.1 * coded_grad
    new_second = 0.999 * second_moment + 0.001 * coded_grad * coded_grad
    first_hat = new_first / (1.0 - 0.9**STEP)
    second_hat = new_second / (1.0 - 0.999**STEP)
    direction = (first_hat / (jnp.sqrt(second_hat) + 1e-08)).astype(BF)
    update = lax.dot_general(
        direction[0], basis, (((1,), (1,)), ((), ())), preferred_element_type=F32
    )
    return (new_first, new_second, update.astype(BF)[None])


def solution(mesh):
    placed = (
        P("dp", "tensor"),
        P(),
        P("dp", "tensor"),
        P("tensor", "dp", None),
        P("tensor", "dp", None),
    )
    return jax.shard_map(
        on_device,
        mesh=mesh,
        in_specs=placed,
        out_specs=(P("tensor", "dp", None), P("tensor", "dp", None), P("tensor", "dp", None)),
        check_vma=False,
    )
```

```python
import functools

import jax
import jax.numpy as jnp
from jax import lax
from jax.experimental import pallas as pl
from jax.experimental.pallas import tpu as pltpu
from jax.sharding import PartitionSpec as P

STEP = 100
BF = jnp.bfloat16
F32 = jnp.float32


def swap(value, axis, bit, count):
    return lax.ppermute(value, axis, [(i, i ^ bit) for i in range(count)])


DEEP = 4


def partial_code_kernel(activations, basis, keep, send, act_buf, basis_buf, total, sems):
    feats = activations.shape[1]
    start = lax.axis_index("tensor") * feats
    step = feats // DEEP
    copies = []
    for k in range(DEEP):
        copies.append(
            pltpu.make_async_copy(
                basis.at[pl.ds(pl.multiple_of(start + k * step, step), step), :],
                basis_buf.at[k],
                sems.at[0, k],
            )
        )
        copies.append(
            pltpu.make_async_copy(
                activations.at[:, pl.ds(k * step, step)], act_buf.at[k], sems.at[1, k]
            )
        )
    for copy in copies:
        copy.start()
    for k in range(DEEP):
        copies[2 * k].wait()
        copies[2 * k + 1].wait()
        part = jnp.dot(act_buf[k], basis_buf[k], preferred_element_type=F32)
        total[...] = part if k == 0 else total[...] + part
    half = keep.shape[0]
    core = lax.rem(lax.axis_index("tensor"), 2)
    keep[...] = total[pl.ds(pl.multiple_of(core * half, half), half), :]
    send[...] = total[pl.ds(pl.multiple_of((1 - core) * half, half), half), :].astype(BF)


def partial_code(activations, basis):
    rows, feats = activations.shape
    rank = basis.shape[1]
    vmem = pl.BlockSpec(memory_space=pltpu.VMEM)
    hbm = pl.BlockSpec(memory_space=pltpu.HBM)
    return pl.pallas_call(
        partial_code_kernel,
        out_shape=(
            jax.ShapeDtypeStruct((rows // 2, rank), F32),
            jax.ShapeDtypeStruct((rows // 2, rank), BF),
        ),
        in_specs=[hbm, hbm],
        out_specs=(vmem, vmem),
        scratch_shapes=[
            pltpu.VMEM((DEEP, rows, feats // DEEP), BF),
            pltpu.VMEM((DEEP, feats // DEEP, rank), BF),
            pltpu.VMEM((rows, rank), F32),
            pltpu.SemaphoreType.DMA((2, DEEP)),
        ],
        compiler_params=pltpu.CompilerParams(vmem_limit_bytes=53 * 2**20),
        cost_estimate=pl.CostEstimate(
            flops=2 * rows * feats * rank,
            bytes_accessed=2 * feats * (rows + rank),
            transcendentals=0,
        ),
        name="partial_code",
    )(activations, basis)


def coded_total(keep, send, n_tensor):
    core = lax.axis_index("tensor") % 2
    total = keep + swap(send, "tensor", 1, n_tensor).astype(F32)
    bit = 2
    while bit < n_tensor:
        total = total + swap(total.astype(BF), "tensor", bit, n_tensor).astype(F32)
        bit *= 2
    mine = total.astype(BF)
    theirs = swap(mine, "tensor", 1, n_tensor)
    return jnp.where(
        core == 0,
        jnp.concatenate([mine, theirs], 0),
        jnp.concatenate([theirs, mine], 0),
    )


def line_total(grad_rows, coded, n_dp, cuts, spare=8):
    rows = grad_rows.shape[0] // n_dp
    d = lax.axis_index("dp")
    z, x = d // 2, d % 2
    first, second = cuts

    def both(block, code, cut):
        split = grad_rows.reshape(n_dp, rows, -1)
        part = lax.dynamic_slice_in_dim(split, block * 2, 2, 0)[:, cut[0] : cut[1]]
        return lax.dot_general(
            part, code, (((2,), (0,)), ((), ())), preferred_element_type=F32
        )

    def term(block, side, code, cut=(0, rows)):
        start = (block * 2 + side) * rows + cut[0]
        part = lax.dynamic_slice_in_dim(grad_rows, start, cut[1] - cut[0], 0)
        return jnp.dot(part, code, preferred_element_type=F32)

    def parity(value, side):
        return lax.dynamic_index_in_dim(value, side, 0, False).astype(F32)

    def hop(value, bit):
        full = [(i, i ^ (2 * bit)) for i in range(n_dp)]
        return lax.ppermute(value.astype(BF), "dp", full)

    def pair(value):
        return swap(value.astype(BF), "dp", 1, n_dp)

    def piece(value, cut):
        return value[cut[0] : cut[1]].astype(F32)

    got2 = pair(term(z ^ 2, 1 - x, coded))
    out1 = both(z ^ 1, coded, (0, first[1] + spare)).astype(BF)
    code, out1 = lax.optimization_barrier((coded, out1))
    near1 = hop(out1, 1)
    n_first = first[1]
    got31 = jnp.concatenate(
        [term(z ^ 3, 1 - x, code, first), term(z ^ 1, 1 - x, code, second)]
    )
    got31 = pair(got31)

    sums = [(term(z ^ 2, x, coded, cut) + piece(got2, cut)).astype(BF) for cut in cuts]
    code, sums = lax.optimization_barrier((coded, sums))
    passed = [hop(part, 1) for part in sums]
    out3 = term(z ^ 3, 1 - x, code, second).astype(BF)
    code, out3, near1 = lax.optimization_barrier((code, out3, near1))
    got3 = pair(out3)
    near1 = near1[:, :n_first]
    own_a = (term(z, 1 - x, code, first) + parity(near1, 1 - x)).astype(BF)
    own_a = jnp.pad(own_a, ((0, 2 * spare), (0, 0)))
    code, own_a = lax.optimization_barrier((coded, own_a))
    own_a = pair(own_a)

    def total(block, cut, code, *parts):
        value = term(block, x, code, cut)
        for part in parts:
            value = value + part.astype(F32)
        return lax.optimization_barrier((code, value.astype(BF)))

    code, total_a = total(z ^ 3, first, code, got31[:n_first], passed[0])
    far_a = hop(total_a, 3)
    code, got31, passed[1] = lax.optimization_barrier((code, got31, passed[1]))
    code, late = total(z ^ 1, second, code, got31[n_first:])
    late = hop(late, 1)
    own_b = pair(term(z, 1 - x, code, second))
    code, total_b = total(z ^ 3, second, code, got3, passed[1])
    far_b = hop(total_b, 3)
    kept = [term(z, x, code, first) + parity(near1, x), term(z, x, code, second)]
    return kept, [(far_a, own_a), (late, far_b, own_b)]


WIDE = 512


def adam_update_kernel(cut, n_terms, n_olds, own, first, second, basis, *refs):
    terms, refs = refs[:n_terms], refs[n_terms + n_olds :]
    new_first, new_second, update = refs[:3]
    first_buf, second_buf, direction, blocks, moment_sem, block_sem = refs[3:]
    here = pl.ds(cut[0], cut[1] - cut[0])
    grad = own[...]
    for term in terms:
        grad = grad + term[: cut[1] - cut[0], :].astype(F32)
    first_buf[...] = 0.9 * first[here, :] + 0.1 * grad
    second_buf[...] = 0.999 * second[here, :] + 0.001 * grad * grad
    moments = [
        pltpu.make_async_copy(first_buf, new_first.at[here, :], moment_sem.at[0]),
        pltpu.make_async_copy(second_buf, new_second.at[here, :], moment_sem.at[1]),
    ]
    for copy in moments:
        copy.start()
    first_hat = first_buf[...] / (1.0 - 0.9**STEP)
    second_hat = second_buf[...] / (1.0 - 0.999**STEP)
    direction[...] = (first_hat / (jnp.sqrt(second_hat) + 1e-08)).astype(BF)

    def out_copy(j):
        return pltpu.make_async_copy(
            blocks.at[j], update.at[here, pl.ds(j * WIDE, WIDE)], block_sem.at[j]
        )

    count = basis.shape[0] // WIDE
    for j in range(count):
        part = lax.dot_general(
            direction[...],
            basis[pl.ds(j * WIDE, WIDE), :],
            (((1,), (1,)), ((), ())),
            preferred_element_type=F32,
        )
        blocks[j] = part.astype(BF)
        out_copy(j).start()
    for j in range(count):
        out_copy(j).wait()
    for copy in moments:
        copy.wait()


def adam_update(cut, own, terms, first, second, basis, olds):
    rows, rank = first.shape
    feats = basis.shape[0]
    here = cut[1] - cut[0]
    vmem = pl.BlockSpec(memory_space=pltpu.VMEM)
    hbm = pl.BlockSpec(memory_space=pl.ANY)
    n_inputs = 4 + len(terms)
    return pl.pallas_call(
        functools.partial(adam_update_kernel, cut, len(terms), len(olds)),
        out_shape=(
            jax.ShapeDtypeStruct((rows, rank), F32),
            jax.ShapeDtypeStruct((rows, rank), F32),
            jax.ShapeDtypeStruct((rows, feats), BF),
        ),
        in_specs=[vmem] * n_inputs + [hbm] * len(olds),
        out_specs=(hbm, hbm, hbm),
        input_output_aliases={n_inputs + i: i for i in range(len(olds))},
        scratch_shapes=[
            pltpu.VMEM((here, rank), F32),
            pltpu.VMEM((here, rank), F32),
            pltpu.VMEM((here, rank), BF),
            pltpu.VMEM((feats // WIDE, here, WIDE), BF),
            pltpu.SemaphoreType.DMA((2,)),
            pltpu.SemaphoreType.DMA((feats // WIDE,)),
        ],
        compiler_params=pltpu.CompilerParams(vmem_limit_bytes=24 * 2**20),
        cost_estimate=pl.CostEstimate(
            flops=2 * here * rank * feats,
            bytes_accessed=2 * here * feats + 2 * rank * feats,
            transcendentals=here * rank,
        ),
        name="adam_update",
    )(own, first, second, basis, *terms, *olds)


def on_device(activations, basis, out_grad, first_moment, second_moment):
    n_tensor = lax.axis_size("tensor")
    n_dp = lax.axis_size("dp")
    keep, send = partial_code(activations, basis)
    coded_rows = coded_total(keep, send, n_tensor)
    if n_dp == 8:
        rows = first_moment.shape[1]
        middle = rows // 32 * 16
        cuts = ((0, middle), (middle, rows))
        kept, others = line_total(out_grad.T, coded_rows, n_dp, cuts)
        outs = ()
        for cut, own, terms in zip(cuts, kept, others):
            outs = adam_update(
                cut, own, terms, first_moment[0], second_moment[0], basis, outs
            )
        return tuple(out[None] for out in outs)
    term = jnp.dot(out_grad.T, coded_rows, preferred_element_type=F32)
    coded_grad = lax.psum_scatter(term, "dp", scatter_dimension=0, tiled=True)[None]
    new_first = 0.9 * first_moment + 0.1 * coded_grad
    new_second = 0.999 * second_moment + 0.001 * coded_grad * coded_grad
    first_hat = new_first / (1.0 - 0.9**STEP)
    second_hat = new_second / (1.0 - 0.999**STEP)
    direction = (first_hat / (jnp.sqrt(second_hat) + 1e-08)).astype(BF)
    update = lax.dot_general(
        direction[0], basis, (((1,), (1,)), ((), ())), preferred_element_type=F32
    )
    return (new_first, new_second, update.astype(BF)[None])


def solution(mesh):
    placed = (
        P("dp", "tensor"),
        P(),
        P("dp", "tensor"),
        P("tensor", "dp", None),
        P("tensor", "dp", None),
    )
    return jax.shard_map(
        on_device,
        mesh=mesh,
        in_specs=placed,
        out_specs=(P("tensor", "dp", None), P("tensor", "dp", None), P("tensor", "dp", None)),
        check_vma=False,
    )
```

```python
import functools

import jax
import jax.numpy as jnp
from jax import lax
from jax.experimental import pallas as pl
from jax.experimental.pallas import tpu as pltpu
from jax.sharding import PartitionSpec as P

STEP = 100
BF = jnp.bfloat16
F32 = jnp.float32


def swap(value, axis, bit, count):
    return lax.ppermute(value, axis, [(i, i ^ bit) for i in range(count)])


DEEP = 8


def partial_code_kernel(activations, basis, keep, send, act_buf, basis_buf, total, sems):
    feats = activations.shape[1]
    start = lax.axis_index("tensor") * feats
    step = feats // DEEP
    copies = []
    for k in range(DEEP):
        copies.append(
            pltpu.make_async_copy(
                basis.at[pl.ds(pl.multiple_of(start + k * step, step), step), :],
                basis_buf.at[k],
                sems.at[0, k],
            )
        )
        copies.append(
            pltpu.make_async_copy(
                activations.at[:, pl.ds(k * step, step)], act_buf.at[k], sems.at[1, k]
            )
        )
    for copy in copies:
        copy.start()
    for k in range(DEEP):
        copies[2 * k].wait()
        copies[2 * k + 1].wait()
        part = jnp.dot(act_buf[k], basis_buf[k], preferred_element_type=F32)
        total[...] = part if k == 0 else total[...] + part
    half = keep.shape[0]
    core = lax.rem(lax.axis_index("tensor"), 2)
    keep[...] = total[pl.ds(pl.multiple_of(core * half, half), half), :]
    send[...] = total[pl.ds(pl.multiple_of((1 - core) * half, half), half), :].astype(BF)


def partial_code(activations, basis):
    rows, feats = activations.shape
    rank = basis.shape[1]
    vmem = pl.BlockSpec(memory_space=pltpu.VMEM)
    hbm = pl.BlockSpec(memory_space=pltpu.HBM)
    return pl.pallas_call(
        partial_code_kernel,
        out_shape=(
            jax.ShapeDtypeStruct((rows // 2, rank), F32),
            jax.ShapeDtypeStruct((rows // 2, rank), BF),
        ),
        in_specs=[hbm, hbm],
        out_specs=(vmem, vmem),
        scratch_shapes=[
            pltpu.VMEM((DEEP, rows, feats // DEEP), BF),
            pltpu.VMEM((DEEP, feats // DEEP, rank), BF),
            pltpu.VMEM((rows, rank), F32),
            pltpu.SemaphoreType.DMA((2, DEEP)),
        ],
        compiler_params=pltpu.CompilerParams(vmem_limit_bytes=53 * 2**20),
        cost_estimate=pl.CostEstimate(
            flops=2 * rows * feats * rank,
            bytes_accessed=2 * feats * (rows + rank),
            transcendentals=0,
        ),
        name="partial_code",
    )(activations, basis)


def coded_total(keep, send, n_tensor):
    core = lax.axis_index("tensor") % 2
    total = keep + swap(send, "tensor", 1, n_tensor).astype(F32)
    bit = 2
    while bit < n_tensor:
        total = total + swap(total.astype(BF), "tensor", bit, n_tensor).astype(F32)
        bit *= 2
    mine = total.astype(BF)
    theirs = swap(mine, "tensor", 1, n_tensor)
    return jnp.where(
        core == 0,
        jnp.concatenate([mine, theirs], 0),
        jnp.concatenate([theirs, mine], 0),
    )


def line_total(grad_rows, coded, n_dp, cuts, spare=8):
    rows = grad_rows.shape[0] // n_dp
    d = lax.axis_index("dp")
    z, x = d // 2, d % 2
    first, second = cuts

    def both(block, code, cut):
        split = grad_rows.reshape(n_dp, rows, -1)
        part = lax.dynamic_slice_in_dim(split, block * 2, 2, 0)[:, cut[0] : cut[1]]
        return lax.dot_general(
            part, code, (((2,), (0,)), ((), ())), preferred_element_type=F32
        )

    def term(block, side, code, cut=(0, rows)):
        start = (block * 2 + side) * rows + cut[0]
        part = lax.dynamic_slice_in_dim(grad_rows, start, cut[1] - cut[0], 0)
        return jnp.dot(part, code, preferred_element_type=F32)

    def parity(value, side):
        return lax.dynamic_index_in_dim(value, side, 0, False).astype(F32)

    def hop(value, bit):
        full = [(i, i ^ (2 * bit)) for i in range(n_dp)]
        return lax.ppermute(value.astype(BF), "dp", full)

    def pair(value):
        return swap(value.astype(BF), "dp", 1, n_dp)

    def piece(value, cut):
        return value[cut[0] : cut[1]].astype(F32)

    def padded(value):
        return jnp.pad(value, ((0, rows - value.shape[0]), (0, 0)))

    got2 = pair(term(z ^ 2, 1 - x, coded))
    out1 = both(z ^ 1, coded, (0, first[1] + spare)).astype(BF)
    code, out1 = lax.optimization_barrier((coded, out1))
    near1 = hop(out1, 1)
    n_first = first[1]
    got31 = jnp.concatenate(
        [term(z ^ 3, 1 - x, code, first), term(z ^ 1, 1 - x, code, second)]
    )
    got31 = pair(got31)

    sums = [(term(z ^ 2, x, coded, cut) + piece(got2, cut)).astype(BF) for cut in cuts]
    code, sums = lax.optimization_barrier((coded, sums))
    passed = [hop(part, 1) for part in sums]
    out3 = term(z ^ 3, 1 - x, code, second).astype(BF)
    code, out3, near1 = lax.optimization_barrier((code, out3, near1))
    got3 = pair(out3)
    near1 = near1[:, : first[1]]
    own_in = (term(z, 1 - x, code) + padded(parity(near1, 1 - x))).astype(BF)
    code, own_in = lax.optimization_barrier((coded, own_in))
    own = pair(own_in)

    def total(block, cut, code, *parts):
        value = term(block, x, code, cut)
        for part in parts:
            value = value + part.astype(F32)
        return lax.optimization_barrier((code, value.astype(BF)))

    code, total_a = total(z ^ 3, first, code, got31[:n_first], passed[0])
    far_a = hop(total_a, 3)
    code, got31, passed[1] = lax.optimization_barrier((code, got31, passed[1]))
    code, late = total(z ^ 1, second, code, got31[n_first:])
    late = hop(late, 1)
    code, total_b = total(z ^ 3, second, code, got3, passed[1])
    far_b = hop(total_b, 3)
    kept = [term(z, x, code, first) + parity(near1, x), term(z, x, code, second)]
    return kept, own, [(far_a,), (late, far_b)]


WIDE = 256


def adam_update_kernel(cut, n_terms, n_olds, own, got, first, second, basis, *refs):
    terms, refs = refs[:n_terms], refs[n_terms + n_olds :]
    new_first, new_second, update = refs[:3]
    first_buf, second_buf, direction, blocks, moment_sem, block_sem = refs[3:]
    here = pl.ds(cut[0], cut[1] - cut[0])
    grad = own[...] + got[here, :].astype(F32)
    for term in terms:
        grad = grad + term[...].astype(F32)
    first_buf[...] = 0.9 * first[here, :] + 0.1 * grad
    second_buf[...] = 0.999 * second[here, :] + 0.001 * grad * grad
    moments = [
        pltpu.make_async_copy(first_buf, new_first.at[here, :], moment_sem.at[0]),
        pltpu.make_async_copy(second_buf, new_second.at[here, :], moment_sem.at[1]),
    ]
    for copy in moments:
        copy.start()
    first_hat = first_buf[...] / (1.0 - 0.9**STEP)
    second_hat = second_buf[...] / (1.0 - 0.999**STEP)
    direction[...] = (first_hat / (jnp.sqrt(second_hat) + 1e-08)).astype(BF)

    def out_copy(j):
        return pltpu.make_async_copy(
            blocks.at[j], update.at[here, pl.ds(j * WIDE, WIDE)], block_sem.at[j]
        )

    count = basis.shape[0] // WIDE
    for j in range(count):
        part = lax.dot_general(
            direction[...],
            basis[pl.ds(j * WIDE, WIDE), :],
            (((1,), (1,)), ((), ())),
            preferred_element_type=F32,
        )
        blocks[j] = part.astype(BF)
        out_copy(j).start()
    for j in range(count):
        out_copy(j).wait()
    for copy in moments:
        copy.wait()


def adam_update(cut, own, got, terms, first, second, basis, olds):
    rows, rank = first.shape
    feats = basis.shape[0]
    here = cut[1] - cut[0]
    vmem = pl.BlockSpec(memory_space=pltpu.VMEM)
    hbm = pl.BlockSpec(memory_space=pl.ANY)
    n_inputs = 5 + len(terms)
    return pl.pallas_call(
        functools.partial(adam_update_kernel, cut, len(terms), len(olds)),
        out_shape=(
            jax.ShapeDtypeStruct((rows, rank), F32),
            jax.ShapeDtypeStruct((rows, rank), F32),
            jax.ShapeDtypeStruct((rows, feats), BF),
        ),
        in_specs=[vmem] * n_inputs + [hbm] * len(olds),
        out_specs=(hbm, hbm, hbm),
        input_output_aliases={n_inputs + i: i for i in range(len(olds))},
        scratch_shapes=[
            pltpu.VMEM((here, rank), F32),
            pltpu.VMEM((here, rank), F32),
            pltpu.VMEM((here, rank), BF),
            pltpu.VMEM((feats // WIDE, here, WIDE), BF),
            pltpu.SemaphoreType.DMA((2,)),
            pltpu.SemaphoreType.DMA((feats // WIDE,)),
        ],
        compiler_params=pltpu.CompilerParams(vmem_limit_bytes=24 * 2**20),
        cost_estimate=pl.CostEstimate(
            flops=2 * here * rank * feats,
            bytes_accessed=2 * here * feats + 2 * rank * feats,
            transcendentals=here * rank,
        ),
        name="adam_update",
    )(own, got, first, second, basis, *terms, *olds)


def on_device(activations, basis, out_grad, first_moment, second_moment):
    n_tensor = lax.axis_size("tensor")
    n_dp = lax.axis_size("dp")
    keep, send = partial_code(activations, basis)
    coded_rows = coded_total(keep, send, n_tensor)
    if n_dp == 8:
        rows = first_moment.shape[1]
        middle = rows // 32 * 16
        cuts = ((0, middle), (middle, rows))
        kept, got, fars = line_total(out_grad.T, coded_rows, n_dp, cuts)
        outs = ()
        for cut, own, terms in zip(cuts, kept, fars):
            outs = adam_update(
                cut, own, got, terms, first_moment[0], second_moment[0], basis, outs
            )
        return tuple(out[None] for out in outs)
    term = jnp.dot(out_grad.T, coded_rows, preferred_element_type=F32)
    coded_grad = lax.psum_scatter(term, "dp", scatter_dimension=0, tiled=True)[None]
    new_first = 0.9 * first_moment + 0.1 * coded_grad
    new_second = 0.999 * second_moment + 0.001 * coded_grad * coded_grad
    first_hat = new_first / (1.0 - 0.9**STEP)
    second_hat = new_second / (1.0 - 0.999**STEP)
    direction = (first_hat / (jnp.sqrt(second_hat) + 1e-08)).astype(BF)
    update = lax.dot_general(
        direction[0], basis, (((1,), (1,)), ((), ())), preferred_element_type=F32
    )
    return (new_first, new_second, update.astype(BF)[None])


def solution(mesh):
    placed = (
        P("dp", "tensor"),
        P(),
        P("dp", "tensor"),
        P("tensor", "dp", None),
        P("tensor", "dp", None),
    )
    return jax.shard_map(
        on_device,
        mesh=mesh,
        in_specs=placed,
        out_specs=(P("tensor", "dp", None), P("tensor", "dp", None), P("tensor", "dp", None)),
        check_vma=False,
    )
```
